256 devices in a mesh: gz: 8 (over y, core), gy: 32 (over z, x).
Axes of the slice: x: 4, y: 4, z: 8, core: 2. Of those that a mesh axis runs over, the one named last changes fastest.
Arguments:
- right_side: float32 [64, 256, 1024], P('gz', 'gy'), may hold values from -5 to 5
- coefficient: float32 [64, 256, 1024], P('gz', 'gy'), may hold values from 0.5 to 4
Outputs:
- correction: float32 [64, 256, 1024], P('gz', 'gy')
- residual: float32 [64, 256, 1024], P('gz', 'gy')
The draws below stay inside these ranges and needn't reach their ends.
All inputs are finite; a program needn't handle non-finite values.
Results may differ from the reference program's by a relative error of at most 0.0003.
Values sent between devices are 32-bit elements; how exact they have to be, the bound alone decides.
A program may use at most 64 MiB of HBM per device.

```python
import math
import jax
import jax.numpy as jnp
from jax import lax

NX = 1024
LEVELS = 4
NZ = 64
NY = 256


def draw_right_side(key, part):
    key = jax.random.fold_in(key, 11)
    phase_key, rough_key = jax.random.split(key)
    shape = (NZ, NY, NX)
    phases = jax.random.uniform(phase_key, (2,), jnp.float32, 0.0, 6.283185307179586)
    zpos = (jnp.arange(NZ, dtype=jnp.float32)[:, None, None] + 0.5) / NZ
    ypos = (jnp.arange(NY, dtype=jnp.float32)[None, :, None] + 0.5) / NY
    xpos = (jnp.arange(NX, dtype=jnp.float32)[None, None, :] + 0.5) / NX
    profile = 0.6 + 0.4 * jnp.sin(6.283185307179586 * ypos + phases[0])
    profile = profile * (0.8 + 0.2 * jnp.cos(6.283185307179586 * xpos + phases[1]))
    profile = profile * (0.7 + 0.3 * jnp.sin(3.141592653589793 * zpos))
    rough = jnp.clip(jax.random.normal(rough_key, shape, jnp.float32), -3.5, 3.5)
    return jnp.clip(rough + 1.5 * profile, -5.0, 5.0)


def block_scale(rng, dims, pieces, least, largest):
    factor_of, own = 1.0, jax.random.fold_in(rng, 6)
    for position, shards_of in pieces:
        draws = jnp.exp(jax.random.uniform(jax.random.fold_in(own, position), (shards_of,), jnp.float32, least / len(pieces), largest / len(pieces)))
        factor_of = factor_of * jnp.repeat(draws, dims[position] // shards_of).reshape([-1 if axis == position else 1 for axis in range(len(dims))])
    return factor_of


def setup_inputs(seed: int = 0) -> dict:
    seeds = jax.random.split(jax.random.key(seed), 3)
    right_side = draw_right_side(jax.random.fold_in(seeds[2], 71), 0)
    coefficient = jnp.clip(jnp.exp(math.log(4.0) - 2.0794415 * jax.random.uniform(seeds[1], (NZ, NY, NX), jnp.float32) ** block_scale(seeds[1], (NZ, NY, NX), ((0, 8), (1, 32)), -0.2, 0.2)), 0.5, 4.0)
    return {"right_side": right_side, "coefficient": coefficient}


def coarsen(field):
    total = field[0::2, 0::2, 0::2] + field[0::2, 0::2, 1::2]
    total = total + field[0::2, 1::2, 0::2] + field[0::2, 1::2, 1::2]
    total = total + field[1::2, 0::2, 0::2] + field[1::2, 0::2, 1::2]
    total = total + field[1::2, 1::2, 0::2] + field[1::2, 1::2, 1::2]
    return total * 0.125


def prolong(field):
    return jnp.repeat(jnp.repeat(jnp.repeat(field, 2, axis=0), 2, axis=1), 2, axis=2)


def face_terms(kpad):
    center = kpad[1:-1, 1:-1, 1:-1]
    z_minus = 0.5 * (center + kpad[:-2, 1:-1, 1:-1])
    z_plus = 0.5 * (center + kpad[2:, 1:-1, 1:-1])
    y_minus = 0.5 * (center + kpad[1:-1, :-2, 1:-1])
    y_plus = 0.5 * (center + kpad[1:-1, 2:, 1:-1])
    x_minus = 0.5 * (center + kpad[1:-1, 1:-1, :-2])
    x_plus = 0.5 * (center + kpad[1:-1, 1:-1, 2:])
    total = z_minus + z_plus + y_minus + y_plus + x_minus + x_plus
    return (z_minus, z_plus, y_minus, y_plus, x_minus, x_plus), total


def neighbour_sum(weights, upad):
    z_minus, z_plus, y_minus, y_plus, x_minus, x_plus = weights
    acc = z_minus * upad[:-2, 1:-1, 1:-1] + z_plus * upad[2:, 1:-1, 1:-1]
    acc = acc + y_minus * upad[1:-1, :-2, 1:-1] + y_plus * upad[1:-1, 2:, 1:-1]
    acc = acc + x_minus * upad[1:-1, 1:-1, :-2] + x_plus * upad[1:-1, 1:-1, 2:]
    return acc


def cycle(rhs, conduct, level):
    scale = 4.0 ** level
    weights, diag = face_terms(jnp.pad(conduct, 1))
    shape = rhs.shape
    parity = (lax.broadcasted_iota(jnp.int32, shape, 0) + lax.broadcasted_iota(jnp.int32, shape, 1)
              + lax.broadcasted_iota(jnp.int32, shape, 2) + 4) % 2

    def smooth(field, sweeps):
        for sweep in range(sweeps):
            for colour in (0, 1):
                fresh = (scale * rhs + neighbour_sum(weights, jnp.pad(field, 1))) / diag
                field = jnp.where(parity == colour, fresh, field)
        return field

    def remainder(field):
        return rhs - (diag * field - neighbour_sum(weights, jnp.pad(field, 1))) / scale

    field = jnp.zeros(shape, jnp.float32)
    if level == LEVELS - 1:
        return smooth(field, 12), None
    field = smooth(field, 2)
    error, unused = cycle(coarsen(remainder(field)), coarsen(conduct), level + 1)
    field = field + prolong(error)
    field = smooth(field, 2)
    return field, remainder(field)


def reference(right_side, coefficient):
    correction, residual = cycle(right_side, coefficient, 0)
    return correction, residual
```

```python
import jax
import jax.numpy as jnp
from jax import lax
from jax.experimental import pallas as pl
from jax.experimental.pallas import tpu as pltpu
from jax.sharding import PartitionSpec as P

MESH = pl.DeviceIdType.MESH
F32 = jnp.float32
T8 = (8, 128)

BUFFERS = dict(
    stage_f=(8, 8), stage_k=(8, 8),
    k0=(2, 10, 20), f0=(2, 8, 16), w0=(2, 6, 8, 16), d0=(2, 8, 16), g0=(2, 8, 16), r0=(10, 20), b0=(10, 20), p0=(10, 20),
    s0=(4, 8),
    c1k=(10, 20), c1f=(10, 20), k1=(2, 10, 20), w1=(2, 6, 8, 16), d1=(2, 8, 16), g1=(2, 8, 16), r1=(10, 20), b1=(10, 20), p1=(10, 20),
    s1=(2, 4),
    m2k=(9, 8), m2f=(9, 8), k2=(2, 20, 2), w2=(2, 6, 18, 2), d2=(2, 18, 2), g2=(2, 18, 2), r2=(20, 2), b2=(20, 2), p2=(20, 2),
    e2v=(10, 2, 2, 3), e2x=(10, 10),
    m3k=(32,), m3f=(32,), k3=(2, 18), w3=(2, 6, 16), d3=(2, 16), g3=(2, 16), r3=(18,), b3=(18,), e3=(40,),
)
ZEROED = ("k0", "f0", "r0", "b0", "p0", "c1k", "c1f", "r1", "b1", "p1", "k2", "r2", "b2", "p2", "e2v", "k3", "r3", "b3", "e3")
GROUPS = ("h0", "k1", "k2", "f1", "f1x", "u0", "u1", "k3", "f2", "f2x", "u2", "f3")


def iota(dim):
    return lax.broadcasted_iota(jnp.int32, T8, dim)


def nearest(d, n, size):
    if d == 0:
        return 0, 0, size
    if d > 0:
        return size - n, -d * size + size - n, n
    return 0, -d * size, n


def loop(first, end, body):
    def shifted(i, c):
        body(i - 8, c)
        return c

    lax.fori_loop(first + 8, end + 8, shifted, 0)


def kernel(nz, ny, f_in, k_in, u_out, r_out, *scratch):
    B = dict(zip(BUFFERS, scratch))
    in_sem, send_sem, recv_sem = scratch[len(BUFFERS):]
    gz, gy = lax.axis_index("gz"), lax.axis_index("gy")
    lane, sub = iota(1), iota(0)
    sent = dict.fromkeys(GROUPS, 0)

    def device(dz, dy):
        return (lax.rem(gz + (dz + nz) % nz, nz), lax.rem(gy + (dy + ny) % ny, ny))

    def pieces(hbm, ref, sem, out):
        copies = []
        for t in range(8):
            here, there = hbm.at[:, :, pl.ds(t * 128, 128)], ref.at[:, t]
            copies.append(pltpu.make_async_copy(there, here, sem) if out else pltpu.make_async_copy(here, there, sem))
        return copies

    def wait_bytes(sem, n):
        view = B["w0"].reshape(1536, 8, 128).at[pl.ds(0, n)]
        pltpu.make_async_copy(view, view, sem).wait()

    for c in pieces(k_in, B["stage_k"], in_sem.at[0], False) + pieces(f_in, B["stage_f"], in_sem.at[1], False):
        c.start()

    for name in ZEROED:
        shape = BUFFERS[name]
        ref = B[name]
        if len(shape) == 3 and shape[0] == 2:
            for i in range(2):
                def clear2(j, c, ref=ref, i=i, shape=shape):
                    ref[i, j] = jnp.zeros(shape[2:] + T8, F32)
                    return c
                lax.fori_loop(0, shape[1], clear2, 0)
        else:
            def clear(j, c, ref=ref, shape=shape):
                if shape[-1] == 3:
                    ref[j] = jnp.zeros((2, 2, 24, 128), F32)
                else:
                    ref[j] = jnp.zeros(shape[1:] + T8, F32)
                return c
            lax.fori_loop(0, shape[0], clear, 0)

    ring = [(a, b) for a in (-1, 0, 1) for b in (-1, 0, 1) if (a, b) != (0, 0)]
    far = [(2, 0), (-2, 0), (0, 2), (0, -2)]
    knights = [(a, b) for a in (-2, -1, 1, 2) for b in (-2, -1, 1, 2) if abs(a) != abs(b)]
    patch = [(a, b) for b in range(-4, 5) for a in range(nz) if (a, b) != (0, 0)]
    line = [b for b in range(1, ny)]
    everyone = patch + [(0, b) for b in line if 4 < b < ny - 4]
    barrier = pltpu.get_barrier_semaphore()
    for dz, dy in everyone:
        pl.semaphore_signal(barrier, inc=1, device_id=device(dz, dy), device_id_type=MESH)

    def put(group, src, dst, n, dz, dy):
        i = GROUPS.index(group)
        sent[group] += n
        pltpu.make_async_remote_copy(
            src_ref=src, dst_ref=dst, send_sem=send_sem.at[i], recv_sem=recv_sem.at[i],
            device_id=device(dz, dy), device_id_type=MESH,
        ).start()

    def received(group):
        wait_bytes(recv_sem.at[GROUPS.index(group)], sent[group])

    def finished(group):
        wait_bytes(send_sem.at[GROUPS.index(group)], sent[group])

    def packed(stage, dst, oq, oy):
        rows = B[stage].reshape(512, 128)
        target = B[dst]

        def body(y, c):
            even = (lane + y) & 1 == 0
            for q in range(4):
                lo = rows[pl.ds(2 * q * 64 + y, 8, stride=8), :]
                hi = rows[pl.ds((2 * q + 1) * 64 + y, 8, stride=8), :]
                target[0, q + oq, y + oy] = jnp.where(even, lo, hi)
                target[1, q + oq, y + oy] = jnp.where(even, hi, lo)
            return c

        lax.fori_loop(0, 8, body, 0)

    wait_bytes(in_sem.at[0], 64)
    packed("stage_k", "k0", 3, 6)
    wait_bytes(in_sem.at[1], 64)
    packed("stage_f", "f0", 2, 4)
    pl.semaphore_wait(barrier, len(everyone))

    def put0(group, name, oq, oy, colours, dz, dy, nq, nyy, skip_q=0):
        sq, tq, lq = nearest(dz, nq, 4)
        sy, ty, ly = nearest(dy, nyy, 8)
        if skip_q:
            lq = nq - skip_q
            if dz < 0:
                sq, tq = sq + skip_q, tq + skip_q
        ref = B[name]
        src, dst = (
            (pl.ds(sq + oq, lq), pl.ds(sy + oy, ly)),
            (pl.ds(tq + oq, lq), pl.ds(ty + oy, ly)),
        )
        if colours:
            put(group, ref.at[(slice(None),) + src], ref.at[(slice(None),) + dst], 2 * lq * ly, dz, dy)
        else:
            put(group, ref.at[src], ref.at[dst], lq * ly, dz, dy)

    def halo0(group, name, oq, oy, colours, depth):
        for dz, dy in ((0, 1), (0, -1), (1, 0), (-1, 0)):
            put0(group, name, oq, oy, colours, dz, dy, (depth + 1) // 2, depth)
        for dz, dy in ((1, 1), (1, -1), (-1, 1), (-1, -1)):
            put0(group, name, oq, oy, colours, dz, dy, 1, depth - 1)
            put0(group, name, oq, oy, colours, dz, dy, 2, depth - 3, 1)

    halo0("h0", "k0", 3, 6, True, 5)
    halo0("h0", "f0", 2, 4, True, 4)

    def put1(group, name, which):
        ref = B[name]
        for dz, dy in which:
            if (dz, dy) in knights:
                sq, tq, lq = nearest(dz, 1, 2)
                sy, ty, ly = nearest(dy, 2, 4)
            else:
                sq, tq, lq = 0, -2 * dz, 2
                sy, ty, ly = 0, -4 * dy, 4
            put(group, ref.at[pl.ds(sq + 4, lq), pl.ds(sy + 8, ly)], ref.at[pl.ds(tq + 4, lq), pl.ds(ty + 8, ly)], lq * ly, dz, dy)

    def coarse1(read, target):
        def body(y1, c):
            even = (lane // 2 + y1) & 1 == 0
            cols = []
            for z1 in range(4):
                t = read(z1, 2 * y1) + read(z1, 2 * y1 + 1)
                cols.append((t + pltpu.roll(t, 127, 1)) * 0.125)
            for q in range(2):
                lo, hi = cols[2 * q], cols[2 * q + 1]
                red, black = jnp.where(even, lo, hi), jnp.where(even, hi, lo)
                target[q + 4, y1 + 8] = jnp.where(lane % 2 == 0, red, pltpu.roll(black, 1, 1))
            return c

        lax.fori_loop(0, 4, body, 0)

    def coarse2(read):
        out = jnp.zeros(T8, F32)
        for y2 in range(2):
            for z2 in range(2):
                t = read(z2, 2 * y2) + read(z2, 2 * y2 + 1)
                t = (t + pltpu.roll(t, 126, 1)) * 0.125
                for j in range(2):
                    v = jnp.take_along_axis(t, (lane % 16) * 8 + 4 * j, axis=1)
                    v = jnp.sum(jnp.where(lane // 16 == sub, v, 0.0), axis=0, keepdims=True)
                    out = jnp.where(sub == y2 * 4 + z2 * 2 + j, jnp.broadcast_to(v, T8), out)
        return out

    k0, c1k, c1f = B["k0"], B["c1k"], B["c1f"]
    coarse1(lambda z, y: k0[0, z + 3, y + 6] + k0[1, z + 3, y + 6], c1k)
    put1("k1", "c1k", ring + far + knights)
    m2k, m2f = B["m2k"], B["m2f"]

    def both1(q, y):
        v = c1k[q + 4, y + 8]
        return v + pltpu.roll(v, 127, 1)

    m2k[4, gz] = coarse2(both1)
    for dz, dy in patch:
        put("k2", m2k.at[4, gz], m2k.at[4 - dy, gz], 1, dz, dy)

    def shifts(v, st, edge):
        a = pltpu.roll(v, st, 1)
        m = jnp.where(lane < st, pltpu.roll(a, 1, 0), a)
        a = pltpu.roll(v, 128 - st, 1)
        p = jnp.where(lane >= 128 - st, pltpu.roll(a, 7, 0), a)
        if edge:
            m = jnp.where((lane < st) & (sub == 0), 0.0, m)
            p = jnp.where((lane >= 128 - st) & (sub == 7), 0.0, p)
        return m, p

    def row_neighbours(ref, qs, y, colour, st, edge):
        at = {q: ref[q, y] for q in range(qs[0] - 1, qs[-1] + 2)}
        low = (lane // st + y + colour) & 1 == 0
        out = []
        for q in qs:
            o = at[q]
            m, p = shifts(o, st, edge)
            out.append((o, jnp.where(low, at[q - 1], at[q + 1]), ref[q, y - 1], ref[q, y + 1], m, p))
        return out

    def weights(own, others):
        diag = 0.5 * (6.0 * own + sum(others[1:], others[0]))
        inverse = jnp.where(own > 0.0, 1.0 / diag, 0.0)
        return inverse, [jnp.where(k > 0.0, 0.5 * (own + k) * inverse, 0.0) for k in others]

    def weigh(level, colour, oq, oy, wq, wy, q0, q1, y0, y1, st):
        k, w, d = B["k%d" % level], B["w%d" % level], B["d%d" % level]

        def body(y, c):
            qs = [q + oq for q in range(q0, q1 + 1)]
            near = row_neighbours(k.at[1 - colour], qs, y + oy, colour, st, True)
            for q, others in zip(qs, near):
                inverse, ws = weights(k[colour, q, y + oy], others)
                d[colour, q - oq + wq, y + wy] = inverse
                for i in range(6):
                    w[colour, i, q - oq + wq, y + wy] = ws[i]
            return c

        loop(y0, y1 + 1, body)

    def fresh(level, colour, qs, y, other, oq, oy, wq, wy, st):
        w, g = B["w%d" % level], B["g%d" % level]
        near = row_neighbours(other, [q + oq for q in qs], y + oy, colour, st, False)
        out = []
        for q, u in zip(qs, near):
            at = (q + wq, y + wy)
            acc = g[(colour,) + at]
            for i in range(6):
                acc = acc + w[(colour, i) + at] * u[i]
            out.append(acc)
        return out

    def half_sweep(level, colour, target, other, q0, q1, y0, y1):
        oq, oy, wq, wy, st = PLACE[level]

        def body(y, c):
            qs = list(range(q0, q1 + 1))
            for q, v in zip(qs, fresh(level, colour, qs, y, other, oq, oy, wq, wy, st)):
                target[q + oq, y + oy] = v
            return c

        loop(y0, y1 + 1, body)

    def residual(level, colour, own, other, qs, y):
        oq, oy, wq, wy, st = PLACE[level]
        d = B["d%d" % level]
        new = fresh(level, colour, qs, y, other, oq, oy, wq, wy, st)
        return [(v - own[q + oq, y + oy]) / (d[colour, q + wq, y + wy] * 4.0**level) for q, v in zip(qs, new)]

    PLACE = {0: (3, 6, 2, 4, 1), 1: (4, 8, 3, 6, 2)}

    received("h0")

    def blank(name, at):
        ref = B[name]
        shape = BUFFERS[name]
        size = [len(range(*a.indices(n))) if isinstance(a, slice) else None for a, n in zip(at, shape)]
        ref[at] = jnp.zeros(tuple(s for s in size if s is not None) + T8, F32)

    ALL = slice(None)
    for side, cut in ((gz == 0, (ALL, slice(0, 3))), (gz == nz - 1, (ALL, slice(7, 10))),
                      (gy == 0, (ALL, ALL, slice(0, 6))), (gy == ny - 1, (ALL, ALL, slice(14, 20)))):
        @pl.when(side)
        def _(cut=cut):
            for colour in range(2):
                if len(cut) == 2:
                    for q in range(cut[1].start, cut[1].stop):
                        blank("k0", (colour, q, slice(0, 20)))
                else:
                    for q in range(10):
                        blank("k0", (colour, q, cut[2]))

    weigh(0, 0, 3, 6, 2, 4, -2, 5, -4, 11, 1)
    weigh(0, 1, 3, 6, 2, 4, -2, 5, -3, 10, 1)
    f0, d0, g0, r0, b0, p0, s0 = (B[n] for n in ("f0", "d0", "g0", "r0", "b0", "p0", "s0"))

    def start0(y, c):
        for q in range(8):
            red = f0[0, q, y] * d0[0, q, y]
            g0[0, q, y] = red
            r0[q + 1, y + 2] = red
        return c

    lax.fori_loop(0, 16, start0, 0)

    def start0b(y, c):
        for q in range(8):
            g0[1, q, y] = f0[1, q, y] * d0[1, q, y]
        return c

    lax.fori_loop(1, 15, start0b, 0)
    half_sweep(0, 1, b0, r0, -2, 5, -3, 10)
    half_sweep(0, 0, r0, b0, -1, 4, -2, 9)
    half_sweep(0, 1, b0, r0, -1, 4, -1, 8)

    def rest0(y, c):
        qs = list(range(4))
        red = residual(0, 0, r0, b0, qs, y)
        black = residual(0, 1, b0, r0, qs, y)
        for q in qs:
            s0[q, y] = red[q] + black[q]
            p0[q + 3, y + 6] = b0[q + 3, y + 6]
        return c

    lax.fori_loop(0, 8, rest0, 0)
    coarse1(lambda z, y: s0[z, y], c1f)
    put1("f1", "c1f", ring)
    put1("f1x", "c1f", far + knights)
    halo0("u0", "p0", 3, 6, False, 5)

    received("k1")
    k1 = B["k1"]
    for side, q_cut, y_cut in ((gz == 0, (0, 4), None), (gz == 1, (0, 2), None), (gz == nz - 1, (6, 10), None), (gz == nz - 2, (8, 10), None),
                               (gy == 0, None, (0, 8)), (gy == 1, None, (0, 4)), (gy == ny - 1, None, (12, 20)), (gy == ny - 2, None, (16, 20))):
        @pl.when(side)
        def _(q_cut=q_cut, y_cut=y_cut):
            for q in range(*(q_cut or (0, 10))):
                blank("c1k", (q, slice(*(y_cut or (0, 20)))))

    def open1(y, c):
        for q in range(10):
            v = c1k[q, y]
            k1[0, q, y] = v
            k1[1, q, y] = pltpu.roll(v, 127, 1)
        return c

    lax.fori_loop(0, 20, open1, 0)
    weigh(1, 0, 4, 8, 3, 6, -3, 4, -6, 9, 2)
    weigh(1, 1, 4, 8, 3, 6, -3, 4, -5, 8, 2)

    received("k2")
    k2, w2, d2, g2, r2, b2, p2 = (B[n] for n in ("k2", "w2", "d2", "g2", "r2", "b2", "p2"))

    def open2(ref, d, y2, zp, j):
        return ref.reshape(576, 128)[pl.ds(d * 64 + y2 * 4 + zp * 2 + j, 8, stride=8), :]

    def fill2(d, c):
        there = gy + d - 4
        inside = jnp.where((there >= 0) & (there < ny), 1.0, 0.0)
        for y2 in range(2):
            for zp in range(2):
                for colour in range(2):
                    k2[colour, 2 * d + y2 + 1, zp] = open2(m2k, d, y2, zp, (colour + y2 + zp) % 2) * inside
        return c

    lax.fori_loop(0, 9, fill2, 0)

    def near2(ref, row, p, zp, colour, edge):
        o, oz = ref[row, zp], ref[row, 1 - zp]
        if (colour + p + zp) % 2 == 0:
            x = pltpu.roll(o, 1, 1)
            x = jnp.where(lane == 0, 0.0, x) if edge else x
        else:
            x = pltpu.roll(o, 127, 1)
            x = jnp.where(lane == 127, 0.0, x) if edge else x
        if zp == 0:
            z = pltpu.roll(oz, 1, 0)
            z = jnp.where(sub == 0, 0.0, z) if edge else z
        else:
            z = pltpu.roll(oz, 7, 0)
            z = jnp.where(sub == 7, 0.0, z) if edge else z
        return (oz, z, ref[row - 1, zp], ref[row + 1, zp], o, x)

    def weigh2(d, c):
        for p in range(2):
            for zp in range(2):
                for colour in range(2):
                    row = 2 * d + p
                    inverse, ws = weights(k2[colour, row + 1, zp], near2(k2.at[1 - colour], row + 1, p, zp, colour, True))
                    d2[colour, row, zp] = inverse
                    for i in range(6):
                        w2[colour, i, row, zp] = ws[i]
        return c

    lax.fori_loop(0, 9, weigh2, 0)

    def fresh2(d, p, zp, colour, other):
        row = 2 * d + p
        u = near2(other, row + 1, p, zp, colour, False)
        acc = g2[colour, row, zp]
        for i in range(6):
            acc = acc + w2[colour, i, row, zp] * u[i]
        return acc

    def half_sweep2(colour, target, other, d0_, d1_):
        def body(d, c):
            for p in range(2):
                for zp in range(2):
                    target[2 * d + p + 1, zp] = fresh2(d, p, zp, colour, other)
            return c

        lax.fori_loop(d0_, d1_ + 1, body, 0)

    m3k, m3f = B["m3k"], B["m3f"]
    total = jnp.zeros(T8, F32)
    for p in range(2):
        for zp in range(2):
            for colour in range(2):
                total = total + k2[colour, 9 + p, zp]
    m3k[gy] = total * 0.125
    for dy in line:
        put("k3", m3k.at[gy], m3k.at[gy], 1, 0, dy)

    received("f1")
    d1, g1, r1, b1, p1, s1 = (B[n] for n in ("d1", "g1", "r1", "b1", "p1", "s1"))

    def start1(q0, q1, y0, y1, write):
        def body(y, c):
            for q in range(q0, q1 + 1):
                v = c1f[q + 4, y + 8]
                red = v * (4.0 * d1[0, q + 3, y + 6])
                g1[0, q + 3, y + 6] = red
                if write:
                    r1[q + 4, y + 8] = red
                g1[1, q + 3, y + 6] = pltpu.roll(v, 127, 1) * (4.0 * d1[1, q + 3, y + 6])
            return c

        loop(y0, y1 + 1, body)

    start1(-2, 3, -4, 7, True)
    half_sweep(1, 1, b1, r1, -2, 3, -3, 6)
    half_sweep(1, 0, r1, b1, -1, 2, -2, 5)
    half_sweep(1, 1, b1, r1, -1, 2, -1, 4)

    def rest1(y, c):
        qs = [0, 1]
        red = residual(1, 0, r1, b1, qs, y)
        black = residual(1, 1, b1, r1, qs, y)
        for q in qs:
            s1[q, y] = red[q] + black[q]
            p1[q + 4, y + 8] = b1[q + 4, y + 8]
        return c

    lax.fori_loop(0, 4, rest1, 0)
    m2f[4, gz] = coarse2(lambda q, y: s1[q, y])
    for dz, dy in patch:
        if abs(dy) <= 2:
            put("f2", m2f.at[4, gz], m2f.at[4 - dy, gz], 1, dz, dy)
    put1("u1", "p1", ring + far + knights)

    received("k3")
    k3, w3, d3, g3, r3, b3, e3 = (B[n] for n in ("k3", "w3", "d3", "g3", "r3", "b3", "e3"))
    even3 = (lane + sub) % 2 == 0
    for m in range(16):
        lo, hi = m3k[2 * m], m3k[2 * m + 1]
        k3[0, m + 1] = jnp.where(even3, lo, hi)
        k3[1, m + 1] = jnp.where(even3, hi, lo)

    def near3(ref, m, colour, edge):
        o = ref[m + 1]
        low = even3 if colour == 0 else jnp.logical_not(even3)
        zm, zp, xm, xp = pltpu.roll(o, 1, 0), pltpu.roll(o, 7, 0), pltpu.roll(o, 1, 1), pltpu.roll(o, 127, 1)
        if edge:
            zm, zp = jnp.where(sub == 0, 0.0, zm), jnp.where(sub == 7, 0.0, zp)
            xm, xp = jnp.where(lane == 0, 0.0, xm), jnp.where(lane == 127, 0.0, xp)
        return (o, jnp.where(low, ref[m], ref[m + 2]), zm, zp, xm, xp)

    def weigh3(m, c):
        for colour in range(2):
            inverse, ws = weights(k3[colour, m + 1], near3(k3.at[1 - colour], m, colour, True))
            d3[colour, m] = inverse * 64.0
            for i in range(6):
                w3[colour, i, m] = ws[i]
        return c

    lax.fori_loop(0, 16, weigh3, 0)

    received("f2")

    def start2(d0_, d1_, write):
        def body(d, c):
            for y2 in range(2):
                for zp in range(2):
                    for colour in range(2):
                        row = 2 * d + y2
                        v = open2(m2f, d, y2, zp, (colour + y2 + zp) % 2) * (16.0 * d2[colour, row, zp])
                        g2[colour, row, zp] = v
                        if write and colour == 0:
                            r2[row + 1, zp] = v
            return c

        lax.fori_loop(d0_, d1_ + 1, body, 0)

    start2(2, 6, True)
    half_sweep2(1, b2, r2, 2, 6)
    half_sweep2(0, r2, b2, 3, 5)
    half_sweep2(1, b2, r2, 3, 5)
    total = jnp.zeros(T8, F32)
    for p in range(2):
        for zp in range(2):
            for colour in range(2):
                own, other = (r2, b2) if colour == 0 else (b2, r2)
                v = fresh2(4, p, zp, colour, other) - own[9 + p, zp]
                total = total + v / (d2[colour, 8 + p, zp] * 16.0)
            p2[9 + p, zp] = b2[9 + p, zp]
    m3f[gy] = total * 0.125
    for dy in line:
        put("f3", m3f.at[gy], m3f.at[gy], 1, 0, dy)
    for dz, dy in patch:
        if abs(dy) > 2:
            put("f2x", m2f.at[4, gz], m2f.at[4 - dy, gz], 1, dz, dy)
    for dy in range(-4, 5):
        if dy:
            put("u2", p2.at[pl.ds(9, 2)], p2.at[pl.ds(9 - 2 * dy, 2)], 4, 0, dy)

    received("f1x")
    start1(-3, 4, -6, 9, False)

    received("f3")
    for m in range(16):
        lo, hi = m3f[2 * m], m3f[2 * m + 1]
        red = jnp.where(even3, lo, hi) * d3[0, m]
        g3[0, m] = red
        r3[m + 1] = red
        g3[1, m] = jnp.where(even3, hi, lo) * d3[1, m]

    def half_sweep3(colour, target, other):
        for m in range(16):
            u = near3(other, m, colour, False)
            acc = g3[colour, m]
            for i in range(6):
                acc = acc + w3[colour, i, m] * u[i]
            target[m + 1] = acc

    half_sweep3(1, b3, r3)

    def sweep3(s, c):
        half_sweep3(0, r3, b3)
        half_sweep3(1, b3, r3)
        return c

    lax.fori_loop(0, 11, sweep3, 0)
    for m in range(16):
        red, black = r3[m + 1], b3[m + 1]
        e3[2 * m + 4] = jnp.where(even3, red, black)
        e3[2 * m + 5] = jnp.where(even3, black, red)

    received("f2x")
    start2(0, 1, False)
    start2(7, 8, False)
    received("u2")
    finished("u2")

    def up2(d, c):
        e = e3[gy + d]
        for p in range(2):
            for zp in range(2):
                p2[2 * d + p + 1, zp] = p2[2 * d + p + 1, zp] + e
        return c

    lax.fori_loop(0, 9, up2, 0)
    half_sweep2(0, r2, p2, 0, 8)
    half_sweep2(1, p2, r2, 1, 7)
    half_sweep2(0, r2, p2, 1, 7)
    half_sweep2(1, p2, r2, 2, 6)

    e2v, e2x = B["e2v"], B["e2x"]

    def store2(d, c):
        for p in range(2):
            for zp in range(2):
                for colour in range(2):
                    ref = r2 if colour == 0 else p2
                    e2v[2 * (d - 2) + p, zp, (colour + p + zp) % 2, pl.ds(8, 8), :] = ref[2 * d + p + 1, zp]
        return c

    lax.fori_loop(2, 7, store2, 0)
    spread = 16 * sub + lane // 8

    def spread2(y2, c):
        for z2 in range(-4, 6):
            parts = []
            for j in range(2):
                row = e2v[y2, z2 % 2, j, pl.ds(8 + gz + z2 // 2, 1), :]
                parts.append(jnp.take_along_axis(jnp.broadcast_to(row, T8), spread, axis=1))
            e2x[z2 + 4, y2] = jnp.where((lane // 4) % 2 == 0, parts[0], parts[1])
        return c

    lax.fori_loop(0, 10, spread2, 0)

    received("u1")
    finished("u1")

    def up1(y2, c):
        for q in range(10):
            e = e2x[q, y2]
            for p in range(2):
                p1[q, 2 * y2 + p] = p1[q, 2 * y2 + p] + e
        return c

    lax.fori_loop(0, 10, up1, 0)
    half_sweep(1, 0, r1, p1, -3, 4, -6, 9)
    half_sweep(1, 1, p1, r1, -3, 4, -5, 8)
    half_sweep(1, 0, r1, p1, -2, 3, -4, 7)
    half_sweep(1, 1, p1, r1, -2, 3, -3, 6)

    received("u0")
    finished("u0")

    def up0(y1, c):
        even = (lane // 2 + y1) & 1 == 0
        for q in range(-2, 4):
            red, black = r1[q + 4, y1 + 8], p1[q + 4, y1 + 8]
            for p in range(2):
                z1 = 2 * q + p
                if -3 <= z1 <= 6:
                    e = jnp.where(even, red, black) if p == 0 else jnp.where(even, black, red)
                    e = jnp.where(lane % 2 == 0, e, pltpu.roll(e, 1, 1))
                    for i in range(2):
                        p0[z1 + 3, 2 * y1 + i + 6] = p0[z1 + 3, 2 * y1 + i + 6] + e
        return c

    loop(-3, 7, up0)
    half_sweep(0, 0, r0, p0, -2, 5, -4, 11)
    half_sweep(0, 1, p0, r0, -2, 5, -3, 10)
    half_sweep(0, 0, r0, p0, -1, 4, -2, 9)
    half_sweep(0, 1, p0, r0, -1, 4, -1, 8)

    out_u, out_r = B["stage_f"].reshape(512, 128), B["stage_k"].reshape(512, 128)

    def finish(y, c):
        even = (lane + y) & 1 == 0
        qs = list(range(4))
        res_red = residual(0, 0, r0, p0, qs, y)
        res_black = residual(0, 1, p0, r0, qs, y)
        for q in qs:
            red, black = r0[q + 3, y + 6], p0[q + 3, y + 6]
            lo, hi = pl.ds(2 * q * 64 + y, 8, stride=8), pl.ds((2 * q + 1) * 64 + y, 8, stride=8)
            out_u[lo, :] = jnp.where(even, red, black)
            out_u[hi, :] = jnp.where(even, black, red)
            out_r[lo, :] = jnp.where(even, res_red[q], res_black[q])
            out_r[hi, :] = jnp.where(even, res_black[q], res_red[q])
        return c

    lax.fori_loop(0, 8, finish, 0)
    for c in pieces(u_out, B["stage_f"], in_sem.at[0], True) + pieces(r_out, B["stage_k"], in_sem.at[1], True):
        c.start()
    for group in GROUPS:
        if group not in ("u0", "u1", "u2"):
            finished(group)
    wait_bytes(in_sem.at[0], 64)
    wait_bytes(in_sem.at[1], 64)


def solution(mesh):
    nz, ny = mesh.shape["gz"], mesh.shape["gy"]

    def on_device(right_side, coefficient):
        out = jax.ShapeDtypeStruct(right_side.shape, F32)

        def body(*refs):
            kernel(nz, ny, *refs)

        scratch = []
        for name, shape in BUFFERS.items():
            if name in ("stage_f", "stage_k"):
                scratch.append(pltpu.VMEM((8, 8, 8, 128), F32))
            elif name == "e2v":
                scratch.append(pltpu.VMEM((10, 2, 2, 24, 128), F32))
            else:
                scratch.append(pltpu.VMEM(shape + T8, F32))
        return pl.pallas_call(
            body,
            out_shape=(out, out),
            in_specs=[pl.BlockSpec(memory_space=pl.ANY)] * 2,
            out_specs=[pl.BlockSpec(memory_space=pl.ANY)] * 2,
            scratch_shapes=scratch
            + [pltpu.SemaphoreType.DMA((2,)), pltpu.SemaphoreType.DMA((len(GROUPS),)), pltpu.SemaphoreType.DMA((len(GROUPS),))],
            compiler_params=pltpu.CompilerParams(collective_id=0, has_side_effects=True, vmem_limit_bytes=56 * 1024 * 1024),
            name="vcycle",
        )(right_side, coefficient)

    placed = (P("gz", "gy", None), P("gz", "gy", None))
    return jax.shard_map(on_device, mesh=mesh, in_specs=placed, out_specs=placed, check_vma=False)
```

```python
import jax
import jax.numpy as jnp
from jax import lax
from jax.experimental import pallas as pl
from jax.experimental.pallas import tpu as pltpu
from jax.sharding import PartitionSpec as P

MESH = pl.DeviceIdType.MESH
F32 = jnp.float32
T8 = (8, 128)

BUFFERS = dict(
    stage_f=(8, 8), stage_k=(8, 8),
    k0=(2, 10, 20), f0=(2, 8, 16), w0=(2, 6, 8, 16), d0=(2, 8, 16), g0=(2, 8, 16), r0=(10, 20), b0=(10, 20), p0=(10, 20),
    s0=(4, 8),
    c1k=(10, 20), c1f=(10, 20), k1=(2, 10, 20), w1=(2, 6, 8, 16), d1=(2, 8, 16), g1=(2, 8, 16), r1=(10, 20), b1=(10, 20), p1=(10, 20),
    s1=(2, 4),
    m2k=(9, 8), m2f=(9, 8), k2=(2, 20, 2), w2=(2, 6, 18, 2), d2=(2, 18, 2), g2=(2, 18, 2), r2=(20, 2), b2=(20, 2), p2=(20, 2),
    e2v=(10, 2, 2, 3), e2x=(10, 10),
    m3k=(32,), m3f=(32,), k3=(2, 18), w3=(2, 6, 16), d3=(2, 16), g3=(2, 16), r3=(18,), b3=(18,), e3=(40,),
)
GROUPS = ("h0", "k1", "k2", "k2x", "f1", "f1x", "u0", "u1", "k3", "f2", "f2x", "u2", "f3")


def iota(dim):
    return lax.broadcasted_iota(jnp.int32, T8, dim)


def nearest(d, n, size):
    if d == 0:
        return 0, 0, size
    if d > 0:
        return size - n, -d * size + size - n, n
    return 0, -d * size, n


def loop(first, end, body, rows=2):
    steps = (end - first) // rows

    def shifted(i, c):
        for n in range(rows):
            body(i * rows + (first + n), c)
        return c

    lax.fori_loop(0, steps, shifted, 0)
    for y in range(first + steps * rows, end):
        body(jnp.int32(y), 0)


def kernel(nz, ny, f_in, k_in, u_out, r_out, *scratch):
    B = dict(zip(BUFFERS, scratch))
    in_sem, send_sem, recv_sem = scratch[len(BUFFERS):]
    gz, gy = lax.axis_index("gz"), lax.axis_index("gy")
    lane, sub = iota(1), iota(0)
    sent = dict.fromkeys(GROUPS, 0)

    def device(dz, dy):
        return (lax.rem(gz + (dz + nz) % nz, nz), lax.rem(gy + (dy + ny) % ny, ny))

    def pieces(hbm, ref, sem, out):
        copies = []
        for t in range(8):
            here, there = hbm.at[:, :, pl.ds(t * 128, 128)], ref.at[:, t]
            copies.append(pltpu.make_async_copy(there, here, sem) if out else pltpu.make_async_copy(here, there, sem))
        return copies

    def wait_bytes(sem, n):
        view = B["w0"].reshape(1536, 8, 128).at[pl.ds(0, n)]
        pltpu.make_async_copy(view, view, sem).wait()

    for c in pieces(k_in, B["stage_k"], in_sem.at[0], False) + pieces(f_in, B["stage_f"], in_sem.at[1], False):
        c.start()

    ring = [(0, 1), (0, -1), (1, 1), (1, -1), (-1, 1), (-1, -1), (1, 0), (-1, 0)]
    far = [(2, 0), (-2, 0), (0, 2), (0, -2)]
    knights = [(a, b) for a in (-2, -1, 1, 2) for b in (-2, -1, 1, 2) if abs(a) != abs(b)]
    patch = [(a, b) for b in (2, -2, 1, -1, 0) for a in range(nz) if (a, b) != (0, 0)]
    line = sorted(range(1, ny), key=lambda b: -min(b, ny - b))
    everyone = patch + [(0, b) for b in line if 2 < b < ny - 2]
    barrier = pltpu.get_barrier_semaphore()
    for dz, dy in everyone:
        pl.semaphore_signal(barrier, inc=1, device_id=device(dz, dy), device_id_type=MESH)

    def put(group, src, dst, n, dz, dy):
        i = GROUPS.index(group)
        sent[group] += n
        pltpu.make_async_remote_copy(
            src_ref=src, dst_ref=dst, send_sem=send_sem.at[i], recv_sem=recv_sem.at[i],
            device_id=device(dz, dy), device_id_type=MESH,
        ).start()

    def received(group):
        wait_bytes(recv_sem.at[GROUPS.index(group)], sent[group])

    def finished(group):
        wait_bytes(send_sem.at[GROUPS.index(group)], sent[group])

    def packed(stage, dst, oq, oy):
        rows = B[stage].reshape(512, 128)
        target = B[dst]

        def body(y, c):
            even = (lane + y) & 1 == 0
            for q in range(4):
                lo = rows[pl.ds(2 * q * 64 + y, 8, stride=8), :]
                hi = rows[pl.ds((2 * q + 1) * 64 + y, 8, stride=8), :]
                target[0, q + oq, y + oy] = jnp.where(even, lo, hi)
                target[1, q + oq, y + oy] = jnp.where(even, hi, lo)
            return c

        loop(0, 8, body)

    wait_bytes(in_sem.at[0], 64)
    packed("stage_k", "k0", 3, 6)
    wait_bytes(in_sem.at[1], 64)
    packed("stage_f", "f0", 2, 4)
    pl.semaphore_wait(barrier, len(everyone))

    covered = {}

    def put0(group, name, oq, oy, colour, dz, dy, nq, nyy, skip_q=0):
        sq, tq, lq = nearest(dz, nq, 4)
        sy, ty, ly = nearest(dy, nyy, 8)
        if skip_q:
            lq = nq - skip_q
            if dz < 0:
                sq, tq = sq + skip_q, tq + skip_q
        if lq <= 0 or ly <= 0:
            return
        ref = B[name] if colour is None else B[name].at[colour]
        covered.setdefault((name, colour), set()).update((tq + i + oq, ty + j + oy) for i in range(lq) for j in range(ly))
        put(group, ref.at[pl.ds(sq + oq, lq), pl.ds(sy + oy, ly)], ref.at[pl.ds(tq + oq, lq), pl.ds(ty + oy, ly)], lq * ly, dz, dy)

    def halo0(group, fields):
        for dz, dy in ((0, 1), (0, -1)):
            for name, oq, oy, colour, depth in fields:
                put0(group, name, oq, oy, colour, dz, dy, 0, depth)
        for dz, dy in ((1, 1), (1, -1), (-1, 1), (-1, -1)):
            for name, oq, oy, colour, depth in fields:
                put0(group, name, oq, oy, colour, dz, dy, 1, depth - 1)
                put0(group, name, oq, oy, colour, dz, dy, 2, depth - 3, 1)
        for dz, dy in ((1, 0), (-1, 0)):
            for name, oq, oy, colour, depth in fields:
                put0(group, name, oq, oy, colour, dz, dy, (depth + 1) // 2, 0)

    halo0("h0", [("k0", 3, 6, 1, 5), ("k0", 3, 6, 0, 4), ("f0", 2, 4, 0, 4), ("f0", 2, 4, 1, 3)])

    def clear(name, index, own, got):
        nq, nyy = BUFFERS[name][-2:]
        have = got | {(own[0] + i, own[1] + j) for i in range(own[2]) for j in range(own[3])}
        for q in range(nq):
            y = 0
            while y < nyy:
                end = y
                while end < nyy and (q, end) not in have:
                    end += 1
                if end > y:
                    B[name][index + (q, slice(y, end))] = jnp.zeros((end - y,) + T8, F32)
                y = end + 1

    def put1(group, name, which):
        ref = B[name]
        for dz, dy in which:
            if (dz, dy) in knights:
                sq, tq, lq = nearest(dz, 1, 2)
                sy, ty, ly = nearest(dy, 2, 4)
            else:
                sq, tq, lq = 0, -2 * dz, 2
                sy, ty, ly = 0, -4 * dy, 4
            covered.setdefault((name, None), set()).update((tq + i + 4, ty + j + 8) for i in range(lq) for j in range(ly))
            put(group, ref.at[pl.ds(sq + 4, lq), pl.ds(sy + 8, ly)], ref.at[pl.ds(tq + 4, lq), pl.ds(ty + 8, ly)], lq * ly, dz, dy)

    def coarse1(read, target):
        def body(y1, c):
            even = (lane // 2 + y1) & 1 == 0
            cols = []
            for z1 in range(4):
                t = read(z1, 2 * y1) + read(z1, 2 * y1 + 1)
                cols.append((t + pltpu.roll(t, 127, 1)) * 0.125)
            for q in range(2):
                lo, hi = cols[2 * q], cols[2 * q + 1]
                red, black = jnp.where(even, lo, hi), jnp.where(even, hi, lo)
                target[q + 4, y1 + 8] = jnp.where(lane % 2 == 0, red, pltpu.roll(black, 1, 1))
            return c

        loop(0, 4, body)

    def coarse2(read):
        out = jnp.zeros(T8, F32)
        for y2 in range(2):
            for z2 in range(2):
                t = read(z2, 2 * y2) + read(z2, 2 * y2 + 1)
                t = (t + pltpu.roll(t, 126, 1)) * 0.125
                for j in range(2):
                    v = jnp.take_along_axis(t, (lane % 16) * 8 + 4 * j, axis=1)
                    v = jnp.sum(jnp.where(lane // 16 == sub, v, 0.0), axis=0, keepdims=True)
                    out = jnp.where(sub == y2 * 4 + z2 * 2 + j, jnp.broadcast_to(v, T8), out)
        return out

    k0, c1k, c1f = B["k0"], B["c1k"], B["c1f"]
    coarse1(lambda z, y: k0[0, z + 3, y + 6] + k0[1, z + 3, y + 6], c1k)
    put1("k1", "c1k", ring + far + knights)
    m2k, m2f = B["m2k"], B["m2f"]

    def both1(q, y):
        v = c1k[q + 4, y + 8]
        return v + pltpu.roll(v, 127, 1)

    m2k[4, gz] = coarse2(both1)
    for dz in range(1, nz):
        put("k2", m2k.at[4, gz], m2k.at[4, gz], 1, dz, 0)

    own0, own1 = (3, 6, 4, 8), (4, 8, 2, 4)
    for colour in range(2):
        clear("k0", (colour,), own0, covered["k0", colour])
        clear("f0", (colour,), (2, 4, 4, 8), covered["f0", colour])
    clear("p0", (), own0, covered["k0", 1])
    for name in ("c1k", "c1f", "p1"):
        clear(name, (), own1, covered["c1k", None])

    def wipe(i, c):
        for name in ("r0", "b0", "r1", "b1"):
            B[name][i] = jnp.zeros((20,) + T8, F32)
        B["e2v"][i] = jnp.zeros((2, 2, 24, 128), F32)
        return c

    lax.fori_loop(0, 10, wipe, 0)
    for row in (0, 19):
        for colour in range(2):
            B["k2"][colour, row] = jnp.zeros((2,) + T8, F32)
        B["p2"][row] = jnp.zeros((2,) + T8, F32)
    for name in ("r2", "b2"):
        B[name][...] = jnp.zeros((20, 2) + T8, F32)
    for m in (0, 17):
        for colour in range(2):
            B["k3"][colour, m] = jnp.zeros(T8, F32)
        B["r3"][m] = jnp.zeros(T8, F32)
        B["b3"][m] = jnp.zeros(T8, F32)
    for m in (0, 36):
        B["e3"][m:m + 4] = jnp.zeros((4,) + T8, F32)

    def open2(ref, d, y2, zp, j):
        return ref.reshape(576, 128)[pl.ds(d * 64 + y2 * 4 + zp * 2 + j, 8, stride=8), :]

    received("k2")
    total = jnp.zeros(T8, F32)
    for n in range(8):
        total = total + open2(m2k, 4, n // 4, n // 2 % 2, n % 2)
    m3k, m3f = B["m3k"], B["m3f"]
    m3k[gy] = total * 0.125
    for dy in (4, -4, 3, -3, 2, -2, 1, -1):
        put("k2x", m2k.at[4], m2k.at[4 - dy], 8, 0, dy)
    for dy in line:
        put("k3", m3k.at[gy], m3k.at[gy], 1, 0, dy)

    def shifts(v, st, edge):
        a = pltpu.roll(v, st, 1)
        m = jnp.where(lane < st, pltpu.roll(a, 1, 0), a)
        a = pltpu.roll(v, 128 - st, 1)
        p = jnp.where(lane >= 128 - st, pltpu.roll(a, 7, 0), a)
        if edge:
            m = jnp.where((lane < st) & (sub == 0), 0.0, m)
            p = jnp.where((lane >= 128 - st) & (sub == 7), 0.0, p)
        return m, p

    def row_neighbours(ref, qs, y, colour, st, edge):
        at = {q: ref[q, y] for q in range(qs[0] - 1, qs[-1] + 2)}
        low = (lane // st + y + colour) & 1 == 0
        out = []
        for q in qs:
            o = at[q]
            m, p = shifts(o, st, edge)
            out.append((o, jnp.where(low, at[q - 1], at[q + 1]), ref[q, y - 1], ref[q, y + 1], m, p))
        return out

    def weights(own, others):
        diag = 0.5 * (6.0 * own + sum(others[1:], others[0]))
        inverse = jnp.where(own > 0.0, 1.0 / diag, 0.0)
        return inverse, [jnp.where(k > 0.0, 0.5 * (own + k) * inverse, 0.0) for k in others]

    def weigh(level, colour, oq, oy, wq, wy, q0, q1, y0, y1, st):
        k, w, d = B["k%d" % level], B["w%d" % level], B["d%d" % level]

        def body(y, c):
            qs = [q + oq for q in range(q0, q1 + 1)]
            near = row_neighbours(k.at[1 - colour], qs, y + oy, colour, st, True)
            for q, others in zip(qs, near):
                inverse, ws = weights(k[colour, q, y + oy], others)
                d[colour, q - oq + wq, y + wy] = inverse
                for i in range(6):
                    w[colour, i, q - oq + wq, y + wy] = ws[i]
            return c

        loop(y0, y1 + 1, body)

    def fresh(level, colour, qs, y, other, oq, oy, wq, wy, st):
        w, g = B["w%d" % level], B["g%d" % level]
        near = row_neighbours(other, [q + oq for q in qs], y + oy, colour, st, False)
        out = []
        for q, u in zip(qs, near):
            at = (q + wq, y + wy)
            acc = g[(colour,) + at]
            for i in range(6):
                acc = acc + w[(colour, i) + at] * u[i]
            out.append(acc)
        return out

    def half_sweep(level, colour, target, other, q0, q1, y0, y1):
        oq, oy, wq, wy, st = PLACE[level]

        qs = list(range(q0, q1 + 1))

        def body(i, c):
            rows = [2 * i + y0, 2 * i + y0 + 1]
            values = [fresh(level, colour, qs, y, other, oq, oy, wq, wy, st) for y in rows]
            for y, row in zip(rows, values):
                for q, v in zip(qs, row):
                    target[q + oq, y + oy] = v
            return c

        lax.fori_loop(0, (y1 + 1 - y0) // 2, body, 0)

    def residual(level, colour, own, other, qs, y):
        oq, oy, wq, wy, st = PLACE[level]
        d = B["d%d" % level]
        new = fresh(level, colour, qs, y, other, oq, oy, wq, wy, st)
        return [(v - own[q + oq, y + oy]) / (d[colour, q + wq, y + wy] * 4.0**level) for q, v in zip(qs, new)]

    PLACE = {0: (3, 6, 2, 4, 1), 1: (4, 8, 3, 6, 2)}

    received("h0")

    def blank(name, at):
        ref = B[name]
        shape = BUFFERS[name]
        size = [len(range(*a.indices(n))) if isinstance(a, slice) else None for a, n in zip(at, shape)]
        ref[at] = jnp.zeros(tuple(s for s in size if s is not None) + T8, F32)

    ALL = slice(None)
    for side, cut in ((gz == 0, (ALL, slice(0, 3))), (gz == nz - 1, (ALL, slice(7, 10))),
                      (gy == 0, (ALL, ALL, slice(0, 6))), (gy == ny - 1, (ALL, ALL, slice(14, 20)))):
        @pl.when(side)
        def _(cut=cut):
            for colour in range(2):
                if len(cut) == 2:
                    for q in range(cut[1].start, cut[1].stop):
                        blank("k0", (colour, q, slice(0, 20)))
                else:
                    for q in range(10):
                        blank("k0", (colour, q, cut[2]))

    weigh(0, 0, 3, 6, 2, 4, -2, 5, -4, 11, 1)
    weigh(0, 1, 3, 6, 2, 4, -2, 5, -3, 10, 1)
    f0, d0, g0, r0, b0, p0, s0 = (B[n] for n in ("f0", "d0", "g0", "r0", "b0", "p0", "s0"))

    def start0(y, c):
        for q in range(8):
            red = f0[0, q, y] * d0[0, q, y]
            g0[0, q, y] = red
            r0[q + 1, y + 2] = red
        return c

    loop(0, 16, start0)

    def start0b(y, c):
        for q in range(8):
            g0[1, q, y] = f0[1, q, y] * d0[1, q, y]
        return c

    loop(1, 15, start0b)
    half_sweep(0, 1, b0, r0, -2, 5, -3, 10)
    half_sweep(0, 0, r0, b0, -1, 4, -2, 9)
    half_sweep(0, 1, b0, r0, -1, 4, -1, 8)

    def rest0(y, c):
        qs = list(range(4))
        red = residual(0, 0, r0, b0, qs, y)
        black = residual(0, 1, b0, r0, qs, y)
        for q in qs:
            s0[q, y] = red[q] + black[q]
            p0[q + 3, y + 6] = b0[q + 3, y + 6]
        return c

    loop(0, 8, rest0)
    coarse1(lambda z, y: s0[z, y], c1f)
    put1("f1", "c1f", ring)
    put1("f1x", "c1f", far + knights)
    halo0("u0", [("p0", 3, 6, None, 5)])

    received("k1")
    k1 = B["k1"]
    for side, q_cut, y_cut in ((gz == 0, (0, 4), None), (gz == 1, (0, 2), None), (gz == nz - 1, (6, 10), None), (gz == nz - 2, (8, 10), None),
                               (gy == 0, None, (0, 8)), (gy == 1, None, (0, 4)), (gy == ny - 1, None, (12, 20)), (gy == ny - 2, None, (16, 20))):
        @pl.when(side)
        def _(q_cut=q_cut, y_cut=y_cut):
            for q in range(*(q_cut or (0, 10))):
                blank("c1k", (q, slice(*(y_cut or (0, 20)))))

    def open1(y, c):
        for q in range(10):
            v = c1k[q, y]
            k1[0, q, y] = v
            k1[1, q, y] = pltpu.roll(v, 127, 1)
        return c

    loop(0, 20, open1)
    weigh(1, 0, 4, 8, 3, 6, -3, 4, -6, 9, 2)
    weigh(1, 1, 4, 8, 3, 6, -3, 4, -5, 8, 2)

    received("k2x")
    k2, w2, d2, g2, r2, b2, p2 = (B[n] for n in ("k2", "w2", "d2", "g2", "r2", "b2", "p2"))

    def fill2(d, c):
        there = gy + d - 4
        inside = jnp.where((there >= 0) & (there < ny), 1.0, 0.0)
        for y2 in range(2):
            for zp in range(2):
                for colour in range(2):
                    k2[colour, 2 * d + y2 + 1, zp] = open2(m2k, d, y2, zp, (colour + y2 + zp) % 2) * inside
        return c

    lax.fori_loop(0, 9, fill2, 0)

    def near2(ref, row, p, zp, colour, edge):
        o, oz = ref[row, zp], ref[row, 1 - zp]
        if (colour + p + zp) % 2 == 0:
            x = pltpu.roll(o, 1, 1)
            x = jnp.where(lane == 0, 0.0, x) if edge else x
        else:
            x = pltpu.roll(o, 127, 1)
            x = jnp.where(lane == 127, 0.0, x) if edge else x
        if zp == 0:
            z = pltpu.roll(oz, 1, 0)
            z = jnp.where(sub == 0, 0.0, z) if edge else z
        else:
            z = pltpu.roll(oz, 7, 0)
            z = jnp.where(sub == 7, 0.0, z) if edge else z
        return (oz, z, ref[row - 1, zp], ref[row + 1, zp], o, x)

    def weigh2(d, c):
        for p in range(2):
            for zp in range(2):
                for colour in range(2):
                    row = 2 * d + p
                    inverse, ws = weights(k2[colour, row + 1, zp], near2(k2.at[1 - colour], row + 1, p, zp, colour, True))
                    d2[colour, row, zp] = inverse
                    for i in range(6):
                        w2[colour, i, row, zp] = ws[i]
        return c

    lax.fori_loop(0, 9, weigh2, 0)

    def fresh2(d, p, zp, colour, other):
        row = 2 * d + p
        u = near2(other, row + 1, p, zp, colour, False)
        acc = g2[colour, row, zp]
        for i in range(6):
            acc = acc + w2[colour, i, row, zp] * u[i]
        return acc

    def half_sweep2(colour, target, other, d0_, d1_):
        def body(d, c):
            for p in range(2):
                for zp in range(2):
                    target[2 * d + p + 1, zp] = fresh2(d, p, zp, colour, other)
            return c

        lax.fori_loop(d0_, d1_ + 1, body, 0)

    received("f1")
    d1, g1, r1, b1, p1, s1 = (B[n] for n in ("d1", "g1", "r1", "b1", "p1", "s1"))

    def start1(q0, q1, y0, y1, write):
        def body(y, c):
            for q in range(q0, q1 + 1):
                v = c1f[q + 4, y + 8]
                red = v * (4.0 * d1[0, q + 3, y + 6])
                g1[0, q + 3, y + 6] = red
                if write:
                    r1[q + 4, y + 8] = red
                g1[1, q + 3, y + 6] = pltpu.roll(v, 127, 1) * (4.0 * d1[1, q + 3, y + 6])
            return c

        loop(y0, y1 + 1, body)

    start1(-2, 3, -4, 7, True)
    half_sweep(1, 1, b1, r1, -2, 3, -3, 6)
    half_sweep(1, 0, r1, b1, -1, 2, -2, 5)
    half_sweep(1, 1, b1, r1, -1, 2, -1, 4)

    def rest1(y, c):
        qs = [0, 1]
        red = residual(1, 0, r1, b1, qs, y)
        black = residual(1, 1, b1, r1, qs, y)
        for q in qs:
            s1[q, y] = red[q] + black[q]
            p1[q + 4, y + 8] = b1[q + 4, y + 8]
        return c

    loop(0, 4, rest1)
    m2f[4, gz] = coarse2(lambda q, y: s1[q, y])
    for dz, dy in patch:
        put("f2", m2f.at[4, gz], m2f.at[4 - dy, gz], 1, dz, dy)
    put1("u1", "p1", ring + far + knights)

    received("k3")
    k3, w3, d3, g3, r3, b3, e3 = (B[n] for n in ("k3", "w3", "d3", "g3", "r3", "b3", "e3"))
    even3 = (lane + sub) % 2 == 0
    for m in range(16):
        lo, hi = m3k[2 * m], m3k[2 * m + 1]
        k3[0, m + 1] = jnp.where(even3, lo, hi)
        k3[1, m + 1] = jnp.where(even3, hi, lo)

    def near3(ref, m, colour, edge):
        o = ref[m + 1]
        low = even3 if colour == 0 else jnp.logical_not(even3)
        zm, zp, xm, xp = pltpu.roll(o, 1, 0), pltpu.roll(o, 7, 0), pltpu.roll(o, 1, 1), pltpu.roll(o, 127, 1)
        if edge:
            zm, zp = jnp.where(sub == 0, 0.0, zm), jnp.where(sub == 7, 0.0, zp)
            xm, xp = jnp.where(lane == 0, 0.0, xm), jnp.where(lane == 127, 0.0, xp)
        return (o, jnp.where(low, ref[m], ref[m + 2]), zm, zp, xm, xp)

    def weigh3(m, c):
        for colour in range(2):
            inverse, ws = weights(k3[colour, m + 1], near3(k3.at[1 - colour], m, colour, True))
            d3[colour, m] = inverse * 64.0
            for i in range(6):
                w3[colour, i, m] = ws[i]
        return c

    lax.fori_loop(0, 16, weigh3, 0)

    received("f2")

    def start2(d0_, d1_, write):
        def body(d, c):
            for y2 in range(2):
                for zp in range(2):
                    for colour in range(2):
                        row = 2 * d + y2
                        v = open2(m2f, d, y2, zp, (colour + y2 + zp) % 2) * (16.0 * d2[colour, row, zp])
                        g2[colour, row, zp] = v
                        if write and colour == 0:
                            r2[row + 1, zp] = v
            return c

        lax.fori_loop(d0_, d1_ + 1, body, 0)

    start2(2, 6, True)
    half_sweep2(1, b2, r2, 2, 6)
    half_sweep2(0, r2, b2, 3, 5)
    half_sweep2(1, b2, r2, 3, 5)
    total = jnp.zeros(T8, F32)
    for p in range(2):
        for zp in range(2):
            for colour in range(2):
                own, other = (r2, b2) if colour == 0 else (b2, r2)
                v = fresh2(4, p, zp, colour, other) - own[9 + p, zp]
                total = total + v / (d2[colour, 8 + p, zp] * 16.0)
            p2[9 + p, zp] = b2[9 + p, zp]
    m3f[gy] = total * 0.125
    for dy in line:
        put("f3", m3f.at[gy], m3f.at[gy], 1, 0, dy)
    for dy in (4, -4, 3, -3):
        put("f2x", m2f.at[4], m2f.at[4 - dy], 8, 0, dy)
    for dy in range(-4, 5):
        if dy:
            put("u2", p2.at[pl.ds(9, 2)], p2.at[pl.ds(9 - 2 * dy, 2)], 4, 0, dy)

    received("f1x")
    start1(-3, 4, -6, 9, False)

    received("f3")
    for m in range(16):
        lo, hi = m3f[2 * m], m3f[2 * m + 1]
        red = jnp.where(even3, lo, hi) * d3[0, m]
        g3[0, m] = red
        r3[m + 1] = red
        g3[1, m] = jnp.where(even3, hi, lo) * d3[1, m]

    def half_sweep3(colour, target, other):
        for m in range(16):
            u = near3(other, m, colour, False)
            acc = g3[colour, m]
            for i in range(6):
                acc = acc + w3[colour, i, m] * u[i]
            target[m + 1] = acc

    half_sweep3(1, b3, r3)

    def sweep3(s, c):
        half_sweep3(0, r3, b3)
        half_sweep3(1, b3, r3)
        return c

    lax.fori_loop(0, 11, sweep3, 0)
    for m in range(16):
        red, black = r3[m + 1], b3[m + 1]
        e3[2 * m + 4] = jnp.where(even3, red, black)
        e3[2 * m + 5] = jnp.where(even3, black, red)

    received("f2x")
    start2(0, 1, False)
    start2(7, 8, False)
    received("u2")
    finished("u2")

    def up2(d, c):
        e = e3[gy + d]
        for p in range(2):
            for zp in range(2):
                p2[2 * d + p + 1, zp] = p2[2 * d + p + 1, zp] + e
        return c

    lax.fori_loop(0, 9, up2, 0)
    half_sweep2(0, r2, p2, 0, 8)
    half_sweep2(1, p2, r2, 1, 7)
    half_sweep2(0, r2, p2, 1, 7)
    half_sweep2(1, p2, r2, 2, 6)

    e2v, e2x = B["e2v"], B["e2x"]

    def store2(d, c):
        for p in range(2):
            for zp in range(2):
                for colour in range(2):
                    ref = r2 if colour == 0 else p2
                    e2v[2 * (d - 2) + p, zp, (colour + p + zp) % 2, pl.ds(8, 8), :] = ref[2 * d + p + 1, zp]
        return c

    lax.fori_loop(2, 7, store2, 0)
    spread = 16 * sub + lane // 8

    def spread2(y2, c):
        for z2 in range(-4, 6):
            parts = []
            for j in range(2):
                row = e2v[y2, z2 % 2, j, pl.ds(8 + gz + z2 // 2, 1), :]
                parts.append(jnp.take_along_axis(jnp.broadcast_to(row, T8), spread, axis=1))
            e2x[z2 + 4, y2] = jnp.where((lane // 4) % 2 == 0, parts[0], parts[1])
        return c

    loop(0, 10, spread2)

    received("u1")
    finished("u1")

    def up1(y2, c):
        for q in range(10):
            e = e2x[q, y2]
            for p in range(2):
                p1[q, 2 * y2 + p] = p1[q, 2 * y2 + p] + e
        return c

    loop(0, 10, up1)
    half_sweep(1, 0, r1, p1, -3, 4, -6, 9)
    half_sweep(1, 1, p1, r1, -3, 4, -5, 8)
    half_sweep(1, 0, r1, p1, -2, 3, -4, 7)
    half_sweep(1, 1, p1, r1, -2, 3, -3, 6)

    received("u0")
    finished("u0")

    def up0(y1, c):
        even = (lane // 2 + y1) & 1 == 0
        for q in range(-2, 4):
            red, black = r1[q + 4, y1 + 8], p1[q + 4, y1 + 8]
            for p in range(2):
                z1 = 2 * q + p
                if -3 <= z1 <= 6:
                    e = jnp.where(even, red, black) if p == 0 else jnp.where(even, black, red)
                    e = jnp.where(lane % 2 == 0, e, pltpu.roll(e, 1, 1))
                    for i in range(2):
                        p0[z1 + 3, 2 * y1 + i + 6] = p0[z1 + 3, 2 * y1 + i + 6] + e
        return c

    loop(-3, 7, up0)
    half_sweep(0, 0, r0, p0, -2, 5, -4, 11)
    half_sweep(0, 1, p0, r0, -2, 5, -3, 10)
    half_sweep(0, 0, r0, p0, -1, 4, -2, 9)
    half_sweep(0, 1, p0, r0, -1, 4, -1, 8)

    out_u, out_r = B["stage_f"].reshape(512, 128), B["stage_k"].reshape(512, 128)

    def finish(y, c):
        even = (lane + y) & 1 == 0
        qs = list(range(4))
        res_red = residual(0, 0, r0, p0, qs, y)
        res_black = residual(0, 1, p0, r0, qs, y)
        for q in qs:
            red, black = r0[q + 3, y + 6], p0[q + 3, y + 6]
            lo, hi = pl.ds(2 * q * 64 + y, 8, stride=8), pl.ds((2 * q + 1) * 64 + y, 8, stride=8)
            out_u[lo, :] = jnp.where(even, red, black)
            out_u[hi, :] = jnp.where(even, black, red)
            out_r[lo, :] = jnp.where(even, res_red[q], res_black[q])
            out_r[hi, :] = jnp.where(even, res_black[q], res_red[q])
        return c

    loop(0, 8, finish)
    for c in pieces(u_out, B["stage_f"], in_sem.at[0], True) + pieces(r_out, B["stage_k"], in_sem.at[1], True):
        c.start()
    for group in GROUPS:
        if group not in ("u0", "u1", "u2"):
            finished(group)
    wait_bytes(in_sem.at[0], 64)
    wait_bytes(in_sem.at[1], 64)


def solution(mesh):
    nz, ny = mesh.shape["gz"], mesh.shape["gy"]

    def on_device(right_side, coefficient):
        out = jax.ShapeDtypeStruct(right_side.shape, F32)

        def body(*refs):
            kernel(nz, ny, *refs)

        scratch = []
        for name, shape in BUFFERS.items():
            if name in ("stage_f", "stage_k"):
                scratch.append(pltpu.VMEM((8, 8, 8, 128), F32))
            elif name == "e2v":
                scratch.append(pltpu.VMEM((10, 2, 2, 24, 128), F32))
            else:
                scratch.append(pltpu.VMEM(shape + T8, F32))
        return pl.pallas_call(
            body,
            out_shape=(out, out),
            in_specs=[pl.BlockSpec(memory_space=pltpu.HBM)] * 2,
            out_specs=[pl.BlockSpec(memory_space=pl.ANY)] * 2,
            scratch_shapes=scratch
            + [pltpu.SemaphoreType.DMA((2,)), pltpu.SemaphoreType.DMA((len(GROUPS),)), pltpu.SemaphoreType.DMA((len(GROUPS),))],
            compiler_params=pltpu.CompilerParams(collective_id=0, has_side_effects=True, vmem_limit_bytes=40 * 1024 * 1024),
            name="vcycle",
        )(right_side, coefficient)

    placed = (P("gz", "gy", None), P("gz", "gy", None))
    return jax.shard_map(on_device, mesh=mesh, in_specs=placed, out_specs=placed, check_vma=False)
```

```python
import jax
import jax.numpy as jnp
from jax import lax
from jax.experimental import pallas as pl
from jax.experimental.pallas import tpu as pltpu
from jax.sharding import PartitionSpec as P

MESH = pl.DeviceIdType.MESH
F32 = jnp.float32
T8 = (8, 128)

BUFFERS = dict(
    stage_f=(8, 8), stage_k=(8, 8),
    k0=(2, 10, 20), f0=(2, 8, 16), w0=(2, 6, 8, 16), d0=(2, 8, 16), g0=(2, 8, 16), r0=(10, 20), b0=(10, 20), p0=(10, 20),
    s0=(4, 8),
    c1k=(10, 20), c1f=(10, 20), k1=(2, 10, 20), w1=(2, 6, 8, 16), d1=(2, 8, 16), g1=(2, 8, 16), r1=(10, 20), b1=(10, 20), p1=(10, 20),
    s1=(2, 4), p1c=(10, 10),
    m2k=(9, 8), m2f=(9, 8), k2=(2, 20, 2), w2=(2, 6, 18, 2), d2=(2, 18, 2), g2=(2, 18, 2), r2=(20, 2), b2=(20, 2), p2=(20, 2),
    e2v=(10, 2, 2, 3), e2x=(10, 10),
    m3k=(32,), m3f=(32,), k3=(2, 18), w3=(2, 6, 16), d3=(2, 16), g3=(2, 16), r3=(18,), b3=(18,), e3=(40,),
)
GROUPS = ("h0z", "h0", "k1", "k2", "k2x", "f1", "f1x", "u0", "u1", "k3", "f2", "f2x", "u2", "f3")


def iota(dim):
    return lax.broadcasted_iota(jnp.int32, T8, dim)


def nearest(d, n, size):
    if d == 0:
        return 0, 0, size
    if d > 0:
        return size - n, -d * size + size - n, n
    return 0, -d * size, n


def loop(first, end, body, rows=2):
    steps = (end - first) // rows

    def shifted(i, c):
        for n in range(rows):
            body(i * rows + (first + n), c)
        return c

    lax.fori_loop(0, steps, shifted, 0)
    for y in range(first + steps * rows, end):
        body(jnp.int32(y), 0)


def kernel(nz, ny, f_in, k_in, u_out, r_out, *scratch):
    B = dict(zip(BUFFERS, scratch))
    in_sem, send_sem, recv_sem = scratch[len(BUFFERS):]
    gz, gy = lax.axis_index("gz"), lax.axis_index("gy")
    lane, sub = iota(1), iota(0)
    sent = dict.fromkeys(GROUPS, 0)

    def device(dz, dy):
        return (lax.rem(gz + (dz + nz) % nz, nz), lax.rem(gy + (dy + ny) % ny, ny))

    def wait_bytes(sem, n):
        view = B["w0"].reshape(1536, 8, 128).at[pl.ds(0, n)]
        pltpu.make_async_copy(view, view, sem).wait()

    pltpu.make_async_copy(k_in, B["stage_k"], in_sem.at[0]).start()
    pltpu.make_async_copy(f_in, B["stage_f"], in_sem.at[1]).start()

    ring = [(0, 1), (0, -1), (1, 1), (1, -1), (-1, 1), (-1, -1), (1, 0), (-1, 0)]
    far = [(2, 0), (-2, 0), (0, 2), (0, -2)]
    knights = [(a, b) for a in (-2, -1, 1, 2) for b in (-2, -1, 1, 2) if abs(a) != abs(b)]
    around = ring + far + knights
    line = sorted(range(1, ny), key=lambda b: -min(b, ny - b))
    patch = [(a, b) for b in (2, -2, 1, -1, 0) for a in range(nz) if (a, b) != (0, 0)]
    everyone = patch + [(0, b) for b in line if 2 < b < ny - 2]
    barrier = pltpu.get_barrier_semaphore()
    for dz, dy in everyone:
        pl.semaphore_signal(barrier, inc=1, device_id=device(dz, dy), device_id_type=MESH)

    def put(group, src, dst, n, dz, dy):
        i = GROUPS.index(group)
        sent[group] += n
        pltpu.make_async_remote_copy(
            src_ref=src, dst_ref=dst, send_sem=send_sem.at[i], recv_sem=recv_sem.at[i],
            device_id=device(dz, dy), device_id_type=MESH,
        ).start()

    def received(group):
        wait_bytes(recv_sem.at[GROUPS.index(group)], sent[group])

    def finished(group):
        wait_bytes(send_sem.at[GROUPS.index(group)], sent[group])

    def packed(stage, dst, oq, oy):
        rows = B[stage].reshape(512, 128)
        target = B[dst]

        def body(y, c):
            even = (lane + y) & 1 == 0
            for q in range(4):
                lo = rows[pl.ds(2 * q * 64 + y, 8, stride=8), :]
                hi = rows[pl.ds((2 * q + 1) * 64 + y, 8, stride=8), :]
                target[0, q + oq, y + oy] = jnp.where(even, lo, hi)
                target[1, q + oq, y + oy] = jnp.where(even, hi, lo)
            return c

        loop(0, 8, body)

    wait_bytes(in_sem.at[0], 64)
    packed("stage_k", "k0", 3, 6)
    wait_bytes(in_sem.at[1], 64)
    packed("stage_f", "f0", 2, 4)
    pl.semaphore_wait(barrier, len(everyone))

    covered = {}

    def put0(group, name, oq, oy, colour, dz, dy, nq, nyy, skip_q=0):
        sq, tq, lq = nearest(dz, nq, 4)
        sy, ty, ly = nearest(dy, nyy, 8)
        if skip_q:
            lq = nq - skip_q
            if dz < 0:
                sq, tq = sq + skip_q, tq + skip_q
        if lq <= 0 or ly <= 0:
            return
        ref = B[name] if colour is None else B[name].at[colour]
        covered.setdefault((name, colour), set()).update((tq + i + oq, ty + j + oy) for i in range(lq) for j in range(ly))
        put(group, ref.at[pl.ds(sq + oq, lq), pl.ds(sy + oy, ly)], ref.at[pl.ds(tq + oq, lq), pl.ds(ty + oy, ly)], lq * ly, dz, dy)

    def halo0(group, fields):
        for dz, dy in ((0, 1), (0, -1)):
            for name, oq, oy, colour, depth in fields:
                put0(group, name, oq, oy, colour, dz, dy, 0, depth)
        for dz, dy in ((1, 0), (-1, 0)):
            for name, oq, oy, colour, depth in fields:
                put0(group + "z" * (group == "h0"), name, oq, oy, colour, dz, dy, (depth + 1) // 2, 0)
        for dz, dy in ((1, 1), (1, -1), (-1, 1), (-1, -1)):
            for name, oq, oy, colour, depth in fields:
                put0(group, name, oq, oy, colour, dz, dy, 1, depth - 1)
                put0(group, name, oq, oy, colour, dz, dy, 2, depth - 3, 1)

    halo0("h0", [("k0", 3, 6, 1, 5), ("k0", 3, 6, 0, 4), ("f0", 2, 4, 0, 4), ("f0", 2, 4, 1, 3)])

    def clear(name, index, own, got):
        nq, nyy = BUFFERS[name][-2:]
        have = got | {(own[0] + i, own[1] + j) for i in range(own[2]) for j in range(own[3])}
        for q in range(nq):
            y = 0
            while y < nyy:
                end = y
                while end < nyy and (q, end) not in have:
                    end += 1
                if end > y:
                    B[name][index + (q, slice(y, end))] = jnp.zeros((end - y,) + T8, F32)
                y = end + 1

    def put1(group, name, which, far_depth, knight_depth, rows, dry=False):
        ref, oy = B[name], 2 * rows
        for dz, dy in which:
            nq, nr = (2, rows) if (dz, dy) in ring else knight_depth if (dz, dy) in knights else far_depth
            sq, tq, lq = nearest(dz, nq, 2)
            sy, ty, ly = nearest(dy, nr, rows)
            if dry:
                covered.setdefault(name, set()).update((tq + i + 4, ty + j + oy) for i in range(lq) for j in range(ly))
            else:
                put(group, ref.at[pl.ds(sq + 4, lq), pl.ds(sy + oy, ly)], ref.at[pl.ds(tq + 4, lq), pl.ds(ty + oy, ly)], lq * ly, dz, dy)

    def coarse1(read, target):
        def body(y1, c):
            even = (lane // 2 + y1) & 1 == 0
            cols = []
            for z1 in range(4):
                t = read(z1, 2 * y1) + read(z1, 2 * y1 + 1)
                cols.append((t + pltpu.roll(t, 127, 1)) * 0.125)
            for q in range(2):
                lo, hi = cols[2 * q], cols[2 * q + 1]
                red, black = jnp.where(even, lo, hi), jnp.where(even, hi, lo)
                target[q + 4, y1 + 8] = jnp.where(lane % 2 == 0, red, pltpu.roll(black, 1, 1))
            return c

        loop(0, 4, body)

    def coarse2(read):
        out = jnp.zeros(T8, F32)
        for y2 in range(2):
            for z2 in range(2):
                t = read(z2, 2 * y2) + read(z2, 2 * y2 + 1)
                t = (t + pltpu.roll(t, 126, 1)) * 0.125
                for j in range(2):
                    v = jnp.take_along_axis(t, (lane % 16) * 8 + 4 * j, axis=1)
                    v = jnp.sum(jnp.where(lane // 16 == sub, v, 0.0), axis=0, keepdims=True)
                    out = jnp.where(sub == y2 * 4 + z2 * 2 + j, jnp.broadcast_to(v, T8), out)
        return out

    k0, c1k, c1f = B["k0"], B["c1k"], B["c1f"]
    coarse1(lambda z, y: k0[0, z + 3, y + 6] + k0[1, z + 3, y + 6], c1k)
    put1("k1", "c1k", around, (2, 3), (1, 2), 4)
    m2k, m2f = B["m2k"], B["m2f"]

    def both1(q, y):
        v = c1k[q + 4, y + 8]
        return v + pltpu.roll(v, 127, 1)

    m2k[4, gz] = coarse2(both1)
    for dz in range(1, nz):
        put("k2", m2k.at[4, gz], m2k.at[4, gz], 1, dz, 0)

    own0, own1 = (3, 6, 4, 8), (4, 8, 2, 4)
    for colour in range(2):
        clear("k0", (colour,), own0, covered["k0", colour])
        clear("f0", (colour,), (2, 4, 4, 8), covered["f0", colour])
    clear("p0", (), own0, covered["k0", 1])
    put1("", "c1k", around, (2, 3), (1, 2), 4, True)
    put1("", "c1f", around, (1, 2), (1, 1), 4, True)
    put1("", "p1c", around, (2, 2), (1, 1), 2, True)
    clear("c1k", (), own1, covered["c1k"])
    clear("c1f", (), own1, covered["c1f"])
    clear("p1c", (), (4, 4, 2, 2), covered["p1c"])

    def wipe(i, c):
        for name in ("r0", "b0", "r1", "b1"):
            B[name][i] = jnp.zeros((20,) + T8, F32)
        B["e2v"][i] = jnp.zeros((2, 2, 24, 128), F32)
        return c

    lax.fori_loop(0, 10, wipe, 0)
    for row in (0, 19):
        for colour in range(2):
            B["k2"][colour, row] = jnp.zeros((2,) + T8, F32)
        B["p2"][row] = jnp.zeros((2,) + T8, F32)
    for name in ("r2", "b2"):
        B[name][...] = jnp.zeros((20, 2) + T8, F32)
    for m in (0, 17):
        for colour in range(2):
            B["k3"][colour, m] = jnp.zeros(T8, F32)
        B["r3"][m] = jnp.zeros(T8, F32)
        B["b3"][m] = jnp.zeros(T8, F32)
    for m in (0, 36):
        B["e3"][m:m + 4] = jnp.zeros((4,) + T8, F32)

    def open2(ref, d, y2, zp, j):
        return ref.reshape(576, 128)[pl.ds(d * 64 + y2 * 4 + zp * 2 + j, 8, stride=8), :]

    received("k2")
    total = jnp.zeros(T8, F32)
    for n in range(8):
        total = total + open2(m2k, 4, n // 4, n // 2 % 2, n % 2)
    m3k, m3f = B["m3k"], B["m3f"]
    m3k[gy] = total * 0.125
    for dy in (4, -4, 3, -3, 2, -2, 1, -1):
        put("k2x", m2k.at[4], m2k.at[4 - dy], 8, 0, dy)
    for dy in line:
        put("k3", m3k.at[gy], m3k.at[gy], 1, 0, dy)

    def shifts(v, st, edge):
        a = pltpu.roll(v, st, 1)
        m = jnp.where(lane < st, pltpu.roll(a, 1, 0), a)
        a = pltpu.roll(v, 128 - st, 1)
        p = jnp.where(lane >= 128 - st, pltpu.roll(a, 7, 0), a)
        if edge:
            m = jnp.where((lane < st) & (sub == 0), 0.0, m)
            p = jnp.where((lane >= 128 - st) & (sub == 7), 0.0, p)
        return m, p

    def row_neighbours(ref, qs, y, colour, st, edge):
        at = {q: ref[q, y] for q in range(qs[0] - 1, qs[-1] + 2)}
        low = (lane // st + y + colour) & 1 == 0
        out = []
        for q in qs:
            o = at[q]
            m, p = shifts(o, st, edge)
            out.append((o, jnp.where(low, at[q - 1], at[q + 1]), ref[q, y - 1], ref[q, y + 1], m, p))
        return out

    def weights(own, others):
        diag = 0.5 * (6.0 * own + sum(others[1:], others[0]))
        inverse = jnp.where(own > 0.0, 1.0 / diag, 0.0)
        return inverse, [jnp.where(k > 0.0, 0.5 * (own + k) * inverse, 0.0) for k in others]

    def weigh(level, colour, oq, oy, wq, wy, q0, q1, y0, y1, st):
        k, w, d = B["k%d" % level], B["w%d" % level], B["d%d" % level]

        def body(y, c):
            qs = [q + oq for q in range(q0, q1 + 1)]
            near = row_neighbours(k.at[1 - colour], qs, y + oy, colour, st, True)
            for q, others in zip(qs, near):
                inverse, ws = weights(k[colour, q, y + oy], others)
                d[colour, q - oq + wq, y + wy] = inverse
                for i in range(6):
                    w[colour, i, q - oq + wq, y + wy] = ws[i]
            return c

        loop(y0, y1 + 1, body)

    def fresh(level, colour, qs, y, other, oq, oy, wq, wy, st):
        w, g = B["w%d" % level], B["g%d" % level]
        near = row_neighbours(other, [q + oq for q in qs], y + oy, colour, st, False)
        out = []
        for q, u in zip(qs, near):
            at = (q + wq, y + wy)
            acc = g[(colour,) + at]
            for i in range(6):
                acc = acc + w[(colour, i) + at] * u[i]
            out.append(acc)
        return out

    def half_sweep(level, colour, target, other, q0, q1, y0, y1):
        oq, oy, wq, wy, st = PLACE[level]

        qs = list(range(q0, q1 + 1))

        def body(i, c):
            rows = [2 * i + y0, 2 * i + y0 + 1]
            values = [fresh(level, colour, qs, y, other, oq, oy, wq, wy, st) for y in rows]
            for y, row in zip(rows, values):
                for q, v in zip(qs, row):
                    target[q + oq, y + oy] = v
            return c

        lax.fori_loop(0, (y1 + 1 - y0) // 2, body, 0)

    def residual(level, colour, own, other, qs, y):
        oq, oy, wq, wy, st = PLACE[level]
        d = B["d%d" % level]
        new = fresh(level, colour, qs, y, other, oq, oy, wq, wy, st)
        return [(v - own[q + oq, y + oy]) / (d[colour, q + wq, y + wy] * 4.0**level) for q, v in zip(qs, new)]

    PLACE = {0: (3, 6, 2, 4, 1), 1: (4, 8, 3, 6, 2)}

    def blank(name, at):
        ref = B[name]
        shape = BUFFERS[name]
        size = [len(range(*a.indices(n))) if isinstance(a, slice) else None for a, n in zip(at, shape)]
        ref[at] = jnp.zeros(tuple(s for s in size if s is not None) + T8, F32)

    def blank0(side, qs, spans):
        @pl.when(side)
        def _():
            for colour in range(2):
                for q in qs:
                    for span in spans:
                        blank("k0", (colour, q, slice(*span)))

    received("h0z")
    blank0(gz == 0, range(0, 3), [(6, 14)])
    blank0(gz == nz - 1, range(7, 10), [(6, 14)])
    weigh(0, 0, 3, 6, 2, 4, -2, 5, 1, 6, 1)
    weigh(0, 1, 3, 6, 2, 4, -2, 5, 1, 6, 1)
    received("h0")
    blank0(gz == 0, range(0, 3), [(0, 6), (14, 20)])
    blank0(gz == nz - 1, range(7, 10), [(0, 6), (14, 20)])
    blank0(gy == 0, range(10), [(0, 6)])
    blank0(gy == ny - 1, range(10), [(14, 20)])
    for ys in ((-1, 0), (7, 8)):
        weigh(0, 0, 3, 6, 2, 4, -2, 5, *ys, 1)
        weigh(0, 1, 3, 6, 2, 4, -2, 5, *ys, 1)
    for ys in ((-3, -2), (9, 10)):
        weigh(0, 0, 3, 6, 2, 4, -1, 4, *ys, 1)
        weigh(0, 1, 3, 6, 2, 4, -1, 4, *ys, 1)
    for y in (-4, 11):
        weigh(0, 0, 3, 6, 2, 4, 0, 3, y, y, 1)
    f0, d0, g0, r0, b0, p0, s0 = (B[n] for n in ("f0", "d0", "g0", "r0", "b0", "p0", "s0"))

    def start0(y, c):
        for q in range(8):
            red = f0[0, q, y] * d0[0, q, y]
            g0[0, q, y] = red
            r0[q + 1, y + 2] = red
        return c

    loop(0, 16, start0)

    def start0b(y, c):
        for q in range(8):
            g0[1, q, y] = f0[1, q, y] * d0[1, q, y]
        return c

    loop(1, 15, start0b)
    half_sweep(0, 1, b0, r0, -2, 5, -3, 10)
    half_sweep(0, 0, r0, b0, -1, 4, -2, 9)
    half_sweep(0, 1, b0, r0, -1, 4, -1, 8)

    def rest0(y, c):
        qs = list(range(4))
        red = residual(0, 0, r0, b0, qs, y)
        black = residual(0, 1, b0, r0, qs, y)
        for q in qs:
            s0[q, y] = red[q] + black[q]
            p0[q + 3, y + 6] = b0[q + 3, y + 6]
        return c

    loop(0, 8, rest0)
    coarse1(lambda z, y: s0[z, y], c1f)
    put1("f1", "c1f", ring, None, None, 4)
    put1("f1x", "c1f", far + knights, (1, 2), (1, 1), 4)
    halo0("u0", [("p0", 3, 6, None, 5)])

    received("k1")
    k1 = B["k1"]
    for side, q_cut, y_cut in ((gz == 0, (0, 4), None), (gz == 1, (0, 2), None), (gz == nz - 1, (6, 10), None), (gz == nz - 2, (8, 10), None),
                               (gy == 0, None, (0, 8)), (gy == 1, None, (0, 4)), (gy == ny - 1, None, (12, 20)), (gy == ny - 2, None, (16, 20))):
        @pl.when(side)
        def _(q_cut=q_cut, y_cut=y_cut):
            for q in range(*(q_cut or (0, 10))):
                blank("c1k", (q, slice(*(y_cut or (0, 20)))))

    def open1(y, c):
        for q in range(10):
            v = c1k[q, y]
            k1[0, q, y] = v
            k1[1, q, y] = pltpu.roll(v, 127, 1)
        return c

    loop(0, 20, open1)
    weigh(1, 0, 4, 8, 3, 6, -3, 4, -6, 9, 2)
    weigh(1, 1, 4, 8, 3, 6, -3, 4, -5, 8, 2)

    received("k2x")
    k2, w2, d2, g2, r2, b2, p2 = (B[n] for n in ("k2", "w2", "d2", "g2", "r2", "b2", "p2"))

    def fill2(d, c):
        there = gy + d - 4
        inside = jnp.where((there >= 0) & (there < ny), 1.0, 0.0)
        for y2 in range(2):
            for zp in range(2):
                for colour in range(2):
                    k2[colour, 2 * d + y2 + 1, zp] = open2(m2k, d, y2, zp, (colour + y2 + zp) % 2) * inside
        return c

    lax.fori_loop(0, 9, fill2, 0)

    def near2(ref, row, p, zp, colour, edge):
        o, oz = ref[row, zp], ref[row, 1 - zp]
        if (colour + p + zp) % 2 == 0:
            x = pltpu.roll(o, 1, 1)
            x = jnp.where(lane == 0, 0.0, x) if edge else x
        else:
            x = pltpu.roll(o, 127, 1)
            x = jnp.where(lane == 127, 0.0, x) if edge else x
        if zp == 0:
            z = pltpu.roll(oz, 1, 0)
            z = jnp.where(sub == 0, 0.0, z) if edge else z
        else:
            z = pltpu.roll(oz, 7, 0)
            z = jnp.where(sub == 7, 0.0, z) if edge else z
        return (oz, z, ref[row - 1, zp], ref[row + 1, zp], o, x)

    def weigh2(d, c):
        for p in range(2):
            for zp in range(2):
                for colour in range(2):
                    row = 2 * d + p
                    inverse, ws = weights(k2[colour, row + 1, zp], near2(k2.at[1 - colour], row + 1, p, zp, colour, True))
                    d2[colour, row, zp] = inverse
                    for i in range(6):
                        w2[colour, i, row, zp] = ws[i]
        return c

    lax.fori_loop(0, 9, weigh2, 0)

    def fresh2(d, p, zp, colour, other):
        row = 2 * d + p
        u = near2(other, row + 1, p, zp, colour, False)
        acc = g2[colour, row, zp]
        for i in range(6):
            acc = acc + w2[colour, i, row, zp] * u[i]
        return acc

    def half_sweep2(colour, target, other, first, last):
        def rows(ds):
            at = [(d, p, zp) for d in ds for p in range(2) for zp in range(2)]
            values = [fresh2(d, p, zp, colour, other) for d, p, zp in at]
            for (d, p, zp), v in zip(at, values):
                target[2 * d + p + 1, zp] = v

        def body(i, c):
            rows([3 * i + first + n for n in range(3)])
            return c

        steps = (last + 1 - first) // 3
        lax.fori_loop(0, steps, body, 0)
        if first + 3 * steps <= last:
            rows(range(first + 3 * steps, last + 1))

    received("f1")
    d1, g1, r1, b1, p1, s1 = (B[n] for n in ("d1", "g1", "r1", "b1", "p1", "s1"))

    def start1(q0, q1, y0, y1, write):
        def body(y, c):
            for q in range(q0, q1 + 1):
                v = c1f[q + 4, y + 8]
                red = v * (4.0 * d1[0, q + 3, y + 6])
                g1[0, q + 3, y + 6] = red
                if write:
                    r1[q + 4, y + 8] = red
                g1[1, q + 3, y + 6] = pltpu.roll(v, 127, 1) * (4.0 * d1[1, q + 3, y + 6])
            return c

        loop(y0, y1 + 1, body)

    start1(-2, 3, -4, 7, True)
    half_sweep(1, 1, b1, r1, -2, 3, -3, 6)
    half_sweep(1, 0, r1, b1, -1, 2, -2, 5)
    half_sweep(1, 1, b1, r1, -1, 2, -1, 4)

    def rest1(y, c):
        qs = [0, 1]
        red = residual(1, 0, r1, b1, qs, y)
        black = residual(1, 1, b1, r1, qs, y)
        for q in qs:
            s1[q, y] = red[q] + black[q]
        return c

    loop(0, 4, rest1)
    m2f[4, gz] = coarse2(lambda q, y: s1[q, y])
    for dz, dy in patch:
        put("f2", m2f.at[4, gz], m2f.at[4 - dy, gz], 1, dz, dy)
    p1c = B["p1c"]
    for q in range(2):
        for y in range(2):
            p1c[q + 4, y + 4] = jnp.where(lane % 2 == 0, b1[q + 4, 2 * y + 8], pltpu.roll(b1[q + 4, 2 * y + 9], 1, 1))
    put1("u1", "p1c", around, (2, 2), (1, 1), 2)

    received("k3")
    k3, w3, d3, g3, r3, b3, e3 = (B[n] for n in ("k3", "w3", "d3", "g3", "r3", "b3", "e3"))
    even3 = (lane + sub) % 2 == 0
    for m in range(16):
        lo, hi = m3k[2 * m], m3k[2 * m + 1]
        k3[0, m + 1] = jnp.where(even3, lo, hi)
        k3[1, m + 1] = jnp.where(even3, hi, lo)

    def near3(ref, m, colour, edge):
        o = ref[m + 1]
        low = even3 if colour == 0 else jnp.logical_not(even3)
        zm, zp, xm, xp = pltpu.roll(o, 1, 0), pltpu.roll(o, 7, 0), pltpu.roll(o, 1, 1), pltpu.roll(o, 127, 1)
        if edge:
            zm, zp = jnp.where(sub == 0, 0.0, zm), jnp.where(sub == 7, 0.0, zp)
            xm, xp = jnp.where(lane == 0, 0.0, xm), jnp.where(lane == 127, 0.0, xp)
        return (o, jnp.where(low, ref[m], ref[m + 2]), zm, zp, xm, xp)

    def weigh3(m, c):
        for colour in range(2):
            inverse, ws = weights(k3[colour, m + 1], near3(k3.at[1 - colour], m, colour, True))
            d3[colour, m] = inverse * 64.0
            for i in range(6):
                w3[colour, i, m] = ws[i]
        return c

    loop(0, 16, weigh3)

    received("f2")

    def start2(d0_, d1_, write):
        def body(d, c):
            for y2 in range(2):
                for zp in range(2):
                    for colour in range(2):
                        row = 2 * d + y2
                        v = open2(m2f, d, y2, zp, (colour + y2 + zp) % 2) * (16.0 * d2[colour, row, zp])
                        g2[colour, row, zp] = v
                        if write and colour == 0:
                            r2[row + 1, zp] = v
            return c

        loop(d0_, d1_ + 1, body)

    start2(2, 6, True)
    half_sweep2(1, b2, r2, 2, 6)
    half_sweep2(0, r2, b2, 3, 5)
    half_sweep2(1, b2, r2, 3, 5)
    total = jnp.zeros(T8, F32)
    for p in range(2):
        for zp in range(2):
            for colour in range(2):
                own, other = (r2, b2) if colour == 0 else (b2, r2)
                v = fresh2(4, p, zp, colour, other) - own[9 + p, zp]
                total = total + v / (d2[colour, 8 + p, zp] * 16.0)
            p2[9 + p, zp] = b2[9 + p, zp]
    m3f[gy] = total * 0.125
    for dy in line:
        put("f3", m3f.at[gy], m3f.at[gy], 1, 0, dy)
    for dy in (4, -4, 3, -3):
        put("f2x", m2f.at[4], m2f.at[4 - dy], 8, 0, dy)
    for dy in range(-4, 5):
        if dy:
            put("u2", p2.at[pl.ds(9, 2)], p2.at[pl.ds(9 - 2 * dy, 2)], 4, 0, dy)

    received("f1x")
    start1(-3, 4, -6, 9, False)

    received("f3")
    for m in range(16):
        lo, hi = m3f[2 * m], m3f[2 * m + 1]
        red = jnp.where(even3, lo, hi) * d3[0, m]
        g3[0, m] = red
        r3[m + 1] = red
        g3[1, m] = jnp.where(even3, hi, lo) * d3[1, m]

    def half_sweep3(colour, target, other):
        for m in range(16):
            u = near3(other, m, colour, False)
            acc = g3[colour, m]
            for i in range(6):
                acc = acc + w3[colour, i, m] * u[i]
            target[m + 1] = acc

    half_sweep3(1, b3, r3)

    def sweep3(s, c):
        half_sweep3(0, r3, b3)
        half_sweep3(1, b3, r3)
        return c

    lax.fori_loop(0, 11, sweep3, 0)
    for m in range(16):
        red, black = r3[m + 1], b3[m + 1]
        e3[2 * m + 4] = jnp.where(even3, red, black)
        e3[2 * m + 5] = jnp.where(even3, black, red)

    received("f2x")
    start2(0, 1, False)
    start2(7, 8, False)
    received("u2")
    finished("u2")

    def up2(d, c):
        e = e3[gy + d]
        for p in range(2):
            for zp in range(2):
                p2[2 * d + p + 1, zp] = p2[2 * d + p + 1, zp] + e
        return c

    loop(0, 9, up2, 3)
    half_sweep2(0, r2, p2, 0, 8)
    half_sweep2(1, p2, r2, 1, 7)
    half_sweep2(0, r2, p2, 1, 7)
    half_sweep2(1, p2, r2, 2, 6)

    e2v, e2x = B["e2v"], B["e2x"]

    def store2(d, c):
        for p in range(2):
            for zp in range(2):
                for colour in range(2):
                    ref = r2 if colour == 0 else p2
                    e2v[2 * (d - 2) + p, zp, (colour + p + zp) % 2, pl.ds(8, 8), :] = ref[2 * d + p + 1, zp]
        return c

    loop(2, 7, store2, 5)
    spread = 16 * sub + lane // 8

    def spread2(y2, c):
        for z2 in range(-4, 6):
            parts = []
            for j in range(2):
                row = e2v[y2, z2 % 2, j, pl.ds(8 + gz + z2 // 2, 1), :]
                parts.append(jnp.take_along_axis(jnp.broadcast_to(row, T8), spread, axis=1))
            e2x[z2 + 4, y2] = jnp.where((lane // 4) % 2 == 0, parts[0], parts[1])
        return c

    loop(0, 10, spread2)

    received("u1")

    def up1(y2, c):
        for q in range(10):
            e = e2x[q, y2]
            for p in range(2):
                p1[q, 2 * y2 + p] = (pltpu.roll(p1c[q, y2], 127, 1) if p else p1c[q, y2]) + e
        return c

    loop(0, 10, up1)
    half_sweep(1, 0, r1, p1, -3, 4, -6, 9)
    half_sweep(1, 1, p1, r1, -3, 4, -5, 8)
    half_sweep(1, 0, r1, p1, -2, 3, -4, 7)
    half_sweep(1, 1, p1, r1, -2, 3, -3, 6)

    received("u0")
    finished("u0")

    def up0(y1, c):
        even = (lane // 2 + y1) & 1 == 0
        for q in range(-2, 4):
            red, black = r1[q + 4, y1 + 8], p1[q + 4, y1 + 8]
            for p in range(2):
                z1 = 2 * q + p
                if -3 <= z1 <= 6:
                    e = jnp.where(even, red, black) if p == 0 else jnp.where(even, black, red)
                    e = jnp.where(lane % 2 == 0, e, pltpu.roll(e, 1, 1))
                    for i in range(2):
                        p0[z1 + 3, 2 * y1 + i + 6] = p0[z1 + 3, 2 * y1 + i + 6] + e
        return c

    loop(-3, 7, up0)
    half_sweep(0, 0, r0, p0, -2, 5, -4, 11)
    half_sweep(0, 1, p0, r0, -2, 5, -3, 10)
    half_sweep(0, 0, r0, p0, -1, 4, -2, 9)
    half_sweep(0, 1, p0, r0, -1, 4, -1, 8)

    out_u, out_r = u_out.reshape(512, 128), r_out.reshape(512, 128)

    def finish(y, c):
        even = (lane + y) & 1 == 0
        qs = list(range(4))
        res_red = residual(0, 0, r0, p0, qs, y)
        res_black = residual(0, 1, p0, r0, qs, y)
        for q in qs:
            red, black = r0[q + 3, y + 6], p0[q + 3, y + 6]
            lo, hi = pl.ds(2 * q * 64 + y, 8, stride=8), pl.ds((2 * q + 1) * 64 + y, 8, stride=8)
            out_u[lo, :] = jnp.where(even, red, black)
            out_u[hi, :] = jnp.where(even, black, red)
            out_r[lo, :] = jnp.where(even, res_red[q], res_black[q])
            out_r[hi, :] = jnp.where(even, res_black[q], res_red[q])
        return c

    loop(0, 8, finish)
    for group in GROUPS:
        if group not in ("u0", "u2"):
            finished(group)


def solution(mesh):
    nz, ny = mesh.shape["gz"], mesh.shape["gy"]

    def on_device(right_side, coefficient):
        depth, rows, width = right_side.shape
        out = jax.ShapeDtypeStruct((depth, width // 128, rows, 128), F32)

        def tiles(array):
            return array.reshape(depth, rows, width // 128, 128).transpose(0, 2, 1, 3)

        def whole(array):
            return array.transpose(0, 2, 1, 3).reshape(depth, rows, width)

        def body(*refs):
            kernel(nz, ny, *refs)

        scratch = []
        for name, shape in BUFFERS.items():
            if name in ("stage_f", "stage_k"):
                scratch.append(pltpu.VMEM((8, 8, 8, 128), F32))
            elif name == "e2v":
                scratch.append(pltpu.VMEM((10, 2, 2, 24, 128), F32))
            else:
                scratch.append(pltpu.VMEM(shape + T8, F32))
        correction, residual = pl.pallas_call(
            body,
            out_shape=(out, out),
            in_specs=[pl.BlockSpec(memory_space=pltpu.HBM)] * 2,
            out_specs=[pl.BlockSpec(memory_space=pltpu.VMEM)] * 2,
            scratch_shapes=scratch
            + [pltpu.SemaphoreType.DMA((2,)), pltpu.SemaphoreType.DMA((len(GROUPS),)), pltpu.SemaphoreType.DMA((len(GROUPS),))],
            compiler_params=pltpu.CompilerParams(collective_id=0, has_side_effects=True, vmem_limit_bytes=40 * 1024 * 1024),
            name="vcycle",
        )(tiles(right_side), tiles(coefficient))
        return whole(correction), whole(residual)

    placed = (P("gz", "gy", None), P("gz", "gy", None))
    return jax.shard_map(on_device, mesh=mesh, in_specs=placed, out_specs=placed, check_vma=False)
```

```python
import jax
import jax.numpy as jnp
from jax import lax
from jax.experimental import pallas as pl
from jax.experimental.pallas import tpu as pltpu
from jax.sharding import PartitionSpec as P

MESH = pl.DeviceIdType.MESH
F32 = jnp.float32
T8 = (8, 128)

BUFFERS = dict(
    stage_f=(8, 8), stage_k=(8, 8),
    k0=(2, 10, 20), f0=(2, 8, 16), w0=(2, 6, 8, 16), d0=(2, 8, 16), g0=(2, 8, 16), r0=(10, 20), b0=(10, 20), p0=(10, 20),
    s0=(4, 8),
    c1k=(10, 20), c1f=(10, 20), k1=(2, 10, 20), w1=(2, 6, 8, 16), d1=(2, 8, 16), g1=(2, 8, 16), r1=(10, 20), b1=(10, 20), p1=(10, 20),
    s1=(2, 4), p1c=(10, 10),
    m2k=(9, 8), m2f=(9, 8), k2=(2, 20, 2), w2=(2, 6, 18, 2), d2=(2, 18, 2), g2=(2, 18, 2), r2=(20, 2), b2=(20, 2), p2=(20, 2),
    e2v=(10, 2, 2, 3), e2x=(10, 10),
    m3k=(32,), m3f=(32,), k3=(2, 18), w3=(2, 6, 16), d3=(2, 16), g3=(2, 16), r3=(18,), b3=(18,), e3=(40,),
)
GROUPS = ("h0z", "h0", "k1", "k2", "k2x", "f1", "f1x", "u0", "u1", "k3", "f2", "f2x", "u2", "f3")


def iota(dim):
    return lax.broadcasted_iota(jnp.int32, T8, dim)


def nearest(d, n, size):
    if d == 0:
        return 0, 0, size
    if d > 0:
        return size - n, -d * size + size - n, n
    return 0, -d * size, n


def loop(first, end, body, rows=2):
    steps = (end - first) // rows

    def shifted(i, c):
        for n in range(rows):
            body(i * rows + (first + n), c)
        return c

    lax.fori_loop(0, steps, shifted, 0)
    for y in range(first + steps * rows, end):
        body(jnp.int32(y), 0)


def kernel(nz, ny, f_in, k_in, u_out, r_out, *scratch):
    B = dict(zip(BUFFERS, scratch))
    in_sem, send_sem, recv_sem = scratch[len(BUFFERS):]
    gz, gy = lax.axis_index("gz"), lax.axis_index("gy")
    lane, sub = iota(1), iota(0)
    sent = dict.fromkeys(GROUPS, 0)

    def device(dz, dy):
        return (lax.rem(gz + (dz + nz) % nz, nz), lax.rem(gy + (dy + ny) % ny, ny))

    def wait_bytes(sem, n):
        view = B["w0"].reshape(1536, 8, 128).at[pl.ds(0, n)]
        pltpu.make_async_copy(view, view, sem).wait()

    pltpu.make_async_copy(k_in, B["stage_k"], in_sem.at[0]).start()
    pltpu.make_async_copy(f_in, B["stage_f"], in_sem.at[1]).start()

    ring = [(0, 1), (0, -1), (1, 1), (1, -1), (-1, 1), (-1, -1), (1, 0), (-1, 0)]
    far = [(2, 0), (-2, 0), (0, 2), (0, -2)]
    knights = [(a, b) for a in (-2, -1, 1, 2) for b in (-2, -1, 1, 2) if abs(a) != abs(b)]
    around = ring + far + knights
    line = sorted(range(1, ny), key=lambda b: -min(b, ny - b))
    patch = [(a, b) for b in (2, -2, 1, -1, 0) for a in range(nz) if (a, b) != (0, 0)]
    everyone = patch + [(0, b) for b in line if 2 < b < ny - 2]
    barrier = pltpu.get_barrier_semaphore()
    for dz, dy in everyone:
        pl.semaphore_signal(barrier, inc=1, device_id=device(dz, dy), device_id_type=MESH)

    def put(group, src, dst, n, dz, dy):
        i = GROUPS.index(group)
        sent[group] += n
        pltpu.make_async_remote_copy(
            src_ref=src, dst_ref=dst, send_sem=send_sem.at[i], recv_sem=recv_sem.at[i],
            device_id=device(dz, dy), device_id_type=MESH,
        ).start()

    def received(group):
        wait_bytes(recv_sem.at[GROUPS.index(group)], sent[group])

    def finished(group):
        wait_bytes(send_sem.at[GROUPS.index(group)], sent[group])

    def packed(stage, dst, oq, oy):
        rows = B[stage].reshape(512, 128)
        target = B[dst]

        def body(y, c):
            even = (lane + y) & 1 == 0
            for q in range(4):
                lo = rows[pl.ds(2 * q * 64 + y, 8, stride=8), :]
                hi = rows[pl.ds((2 * q + 1) * 64 + y, 8, stride=8), :]
                target[0, q + oq, y + oy] = jnp.where(even, lo, hi)
                target[1, q + oq, y + oy] = jnp.where(even, hi, lo)
            return c

        loop(0, 8, body)

    wait_bytes(in_sem.at[0], 64)
    packed("stage_k", "k0", 3, 6)
    wait_bytes(in_sem.at[1], 64)
    packed("stage_f", "f0", 2, 4)
    pl.semaphore_wait(barrier, len(everyone))

    covered = {}

    def put0(group, name, oq, oy, colour, dz, dy, nq, nyy, skip_q=0):
        sq, tq, lq = nearest(dz, nq, 4)
        sy, ty, ly = nearest(dy, nyy, 8)
        if skip_q:
            lq = nq - skip_q
            if dz < 0:
                sq, tq = sq + skip_q, tq + skip_q
        if lq <= 0 or ly <= 0:
            return
        ref = B[name] if colour is None else B[name].at[colour]
        covered.setdefault((name, colour), set()).update((tq + i + oq, ty + j + oy) for i in range(lq) for j in range(ly))
        put(group, ref.at[pl.ds(sq + oq, lq), pl.ds(sy + oy, ly)], ref.at[pl.ds(tq + oq, lq), pl.ds(ty + oy, ly)], lq * ly, dz, dy)

    def halo0(group, fields):
        for dz, dy in ((0, 1), (0, -1)):
            for name, oq, oy, colour, depth in fields:
                put0(group, name, oq, oy, colour, dz, dy, 0, depth)
        for dz, dy in ((1, 0), (-1, 0)):
            for name, oq, oy, colour, depth in fields:
                put0(group + "z" * (group == "h0"), name, oq, oy, colour, dz, dy, (depth + 1) // 2, 0)
        for dz, dy in ((1, 1), (1, -1), (-1, 1), (-1, -1)):
            for name, oq, oy, colour, depth in fields:
                put0(group, name, oq, oy, colour, dz, dy, 1, depth - 1)
                put0(group, name, oq, oy, colour, dz, dy, 2, depth - 3, 1)

    halo0("h0", [("k0", 3, 6, 1, 5), ("k0", 3, 6, 0, 4), ("f0", 2, 4, 0, 4), ("f0", 2, 4, 1, 3)])

    def clear(name, index, own, got):
        nq, nyy = BUFFERS[name][-2:]
        have = got | {(own[0] + i, own[1] + j) for i in range(own[2]) for j in range(own[3])}
        for q in range(nq):
            y = 0
            while y < nyy:
                end = y
                while end < nyy and (q, end) not in have:
                    end += 1
                if end > y:
                    B[name][index + (q, slice(y, end))] = jnp.zeros((end - y,) + T8, F32)
                y = end + 1

    def put1(group, name, which, far_depth, knight_depth, rows, dry=False):
        ref, oy = B[name], 2 * rows
        for dz, dy in which:
            nq, nr = (2, rows) if (dz, dy) in ring else knight_depth if (dz, dy) in knights else far_depth
            sq, tq, lq = nearest(dz, nq, 2)
            sy, ty, ly = nearest(dy, nr, rows)
            if dry:
                covered.setdefault(name, set()).update((tq + i + 4, ty + j + oy) for i in range(lq) for j in range(ly))
            else:
                put(group, ref.at[pl.ds(sq + 4, lq), pl.ds(sy + oy, ly)], ref.at[pl.ds(tq + 4, lq), pl.ds(ty + oy, ly)], lq * ly, dz, dy)

    def coarse1(read, target):
        def body(y1, c):
            even = (lane // 2 + y1) & 1 == 0
            cols = []
            for z1 in range(4):
                t = read(z1, 2 * y1) + read(z1, 2 * y1 + 1)
                cols.append((t + pltpu.roll(t, 127, 1)) * 0.125)
            for q in range(2):
                lo, hi = cols[2 * q], cols[2 * q + 1]
                red, black = jnp.where(even, lo, hi), jnp.where(even, hi, lo)
                target[q + 4, y1 + 8] = jnp.where(lane % 2 == 0, red, pltpu.roll(black, 1, 1))
            return c

        loop(0, 4, body)

    def coarse2(read):
        out = jnp.zeros(T8, F32)
        for y2 in range(2):
            for z2 in range(2):
                t = read(z2, 2 * y2) + read(z2, 2 * y2 + 1)
                t = (t + pltpu.roll(t, 126, 1)) * 0.125
                for j in range(2):
                    v = jnp.take_along_axis(t, (lane % 16) * 8 + 4 * j, axis=1)
                    v = jnp.sum(jnp.where(lane // 16 == sub, v, 0.0), axis=0, keepdims=True)
                    out = jnp.where(sub == y2 * 4 + z2 * 2 + j, jnp.broadcast_to(v, T8), out)
        return out

    k0, c1k, c1f = B["k0"], B["c1k"], B["c1f"]
    coarse1(lambda z, y: k0[0, z + 3, y + 6] + k0[1, z + 3, y + 6], c1k)
    m2k, m2f = B["m2k"], B["m2f"]

    def both1(q, y):
        v = c1k[q + 4, y + 8]
        return v + pltpu.roll(v, 127, 1)

    m2k[4, gz] = coarse2(both1)
    for dz in range(1, nz):
        put("k2", m2k.at[4, gz], m2k.at[4, gz], 1, dz, 0)

    own0, own1 = (3, 6, 4, 8), (4, 8, 2, 4)
    for colour in range(2):
        clear("k0", (colour,), own0, covered["k0", colour])
        clear("f0", (colour,), (2, 4, 4, 8), covered["f0", colour])
    clear("p0", (), own0, covered["k0", 1])
    put1("", "c1k", around, (2, 3), (1, 2), 4, True)
    put1("", "c1f", around, (1, 2), (1, 1), 4, True)
    put1("", "p1c", around, (2, 2), (1, 1), 2, True)
    clear("c1k", (), own1, covered["c1k"])
    clear("c1f", (), own1, covered["c1f"])
    clear("p1c", (), (4, 4, 2, 2), covered["p1c"])

    def wipe(i, c):
        for name in ("r0", "b0", "r1", "b1"):
            B[name][i] = jnp.zeros((20,) + T8, F32)
        B["e2v"][i] = jnp.zeros((2, 2, 24, 128), F32)
        return c

    lax.fori_loop(0, 10, wipe, 0)
    for row in (0, 19):
        for colour in range(2):
            B["k2"][colour, row] = jnp.zeros((2,) + T8, F32)
        B["p2"][row] = jnp.zeros((2,) + T8, F32)
    for name in ("r2", "b2"):
        B[name][...] = jnp.zeros((20, 2) + T8, F32)
    for m in (0, 17):
        for colour in range(2):
            B["k3"][colour, m] = jnp.zeros(T8, F32)
        B["r3"][m] = jnp.zeros(T8, F32)
        B["b3"][m] = jnp.zeros(T8, F32)
    for m in (0, 36):
        B["e3"][m:m + 4] = jnp.zeros((4,) + T8, F32)

    def open2(ref, d, y2, zp, j):
        return ref.reshape(576, 128)[pl.ds(d * 64 + y2 * 4 + zp * 2 + j, 8, stride=8), :]

    def shifts(v, st, edge):
        a = pltpu.roll(v, st, 1)
        m = jnp.where(lane < st, pltpu.roll(a, 1, 0), a)
        a = pltpu.roll(v, 128 - st, 1)
        p = jnp.where(lane >= 128 - st, pltpu.roll(a, 7, 0), a)
        if edge:
            m = jnp.where((lane < st) & (sub == 0), 0.0, m)
            p = jnp.where((lane >= 128 - st) & (sub == 7), 0.0, p)
        return m, p

    def row_neighbours(ref, qs, y, colour, st, edge):
        at = {q: ref[q, y] for q in range(qs[0] - 1, qs[-1] + 2)}
        low = (lane // st + y + colour) & 1 == 0
        out = []
        for q in qs:
            o = at[q]
            m, p = shifts(o, st, edge)
            out.append((o, jnp.where(low, at[q - 1], at[q + 1]), ref[q, y - 1], ref[q, y + 1], m, p))
        return out

    def weights(own, others):
        diag = 0.5 * (6.0 * own + sum(others[1:], others[0]))
        inverse = jnp.where(own > 0.0, 1.0 / diag, 0.0)
        return inverse, [jnp.where(k > 0.0, 0.5 * (own + k) * inverse, 0.0) for k in others]

    def weigh(level, colour, oq, oy, wq, wy, q0, q1, y0, y1, st):
        k, w, d = B["k%d" % level], B["w%d" % level], B["d%d" % level]

        def body(y, c):
            qs = [q + oq for q in range(q0, q1 + 1)]
            near = row_neighbours(k.at[1 - colour], qs, y + oy, colour, st, True)
            for q, others in zip(qs, near):
                inverse, ws = weights(k[colour, q, y + oy], others)
                d[colour, q - oq + wq, y + wy] = inverse
                for i in range(6):
                    w[colour, i, q - oq + wq, y + wy] = ws[i]
            return c

        loop(y0, y1 + 1, body)

    def fresh(level, colour, qs, y, other, oq, oy, wq, wy, st):
        w, g = B["w%d" % level], B["g%d" % level]
        near = row_neighbours(other, [q + oq for q in qs], y + oy, colour, st, False)
        out = []
        for q, u in zip(qs, near):
            at = (q + wq, y + wy)
            acc = g[(colour,) + at]
            for i in range(6):
                acc = acc + w[(colour, i) + at] * u[i]
            out.append(acc)
        return out

    def half_sweep(level, colour, target, other, q0, q1, y0, y1):
        oq, oy, wq, wy, st = PLACE[level]

        qs = list(range(q0, q1 + 1))

        def rows(ys):
            values = [fresh(level, colour, qs, y, other, oq, oy, wq, wy, st) for y in ys]
            for y, row in zip(ys, values):
                for q, v in zip(qs, row):
                    target[q + oq, y + oy] = v

        def body(i, c):
            rows([4 * i + y0 + n for n in range(4)])
            return c

        steps = (y1 + 1 - y0) // 4
        lax.fori_loop(0, steps, body, 0)
        if y0 + 4 * steps <= y1:
            rows(range(y0 + 4 * steps, y1 + 1))

    def residual(level, colour, own, other, qs, y):
        oq, oy, wq, wy, st = PLACE[level]
        d = B["d%d" % level]
        new = fresh(level, colour, qs, y, other, oq, oy, wq, wy, st)
        return [(v - own[q + oq, y + oy]) / (d[colour, q + wq, y + wy] * 4.0**level) for q, v in zip(qs, new)]

    PLACE = {0: (3, 6, 2, 4, 1), 1: (4, 8, 3, 6, 2)}

    def blank(name, at):
        ref = B[name]
        shape = BUFFERS[name]
        size = [len(range(*a.indices(n))) if isinstance(a, slice) else None for a, n in zip(at, shape)]
        ref[at] = jnp.zeros(tuple(s for s in size if s is not None) + T8, F32)

    def blank0(side, qs, spans):
        @pl.when(side)
        def _():
            for colour in range(2):
                for q in qs:
                    for span in spans:
                        blank("k0", (colour, q, slice(*span)))

    f0, d0, g0, r0, b0, p0, s0 = (B[n] for n in ("f0", "d0", "g0", "r0", "b0", "p0", "s0"))

    def start0(y, c):
        for q in range(8):
            red = f0[0, q, y] * d0[0, q, y]
            g0[0, q, y] = red
            r0[q + 1, y + 2] = red
        return c


    def start0b(y, c):
        for q in range(8):
            g0[1, q, y] = f0[1, q, y] * d0[1, q, y]
        return c

    received("h0z")
    blank0(gz == 0, range(0, 3), [(6, 14)])
    blank0(gz == nz - 1, range(7, 10), [(6, 14)])
    weigh(0, 0, 3, 6, 2, 4, -2, 5, 1, 6, 1)
    weigh(0, 1, 3, 6, 2, 4, -2, 5, 1, 6, 1)
    loop(5, 11, start0)
    loop(5, 11, start0b)
    put1("k1", "c1k", around, (2, 3), (1, 2), 4)
    received("h0")
    blank0(gz == 0, range(0, 3), [(0, 6), (14, 20)])
    blank0(gz == nz - 1, range(7, 10), [(0, 6), (14, 20)])
    blank0(gy == 0, range(10), [(0, 6)])
    blank0(gy == ny - 1, range(10), [(14, 20)])
    for ys in ((-1, 0), (7, 8)):
        weigh(0, 0, 3, 6, 2, 4, -2, 5, *ys, 1)
        weigh(0, 1, 3, 6, 2, 4, -2, 5, *ys, 1)
    for ys in ((-3, -2), (9, 10)):
        weigh(0, 0, 3, 6, 2, 4, -1, 4, *ys, 1)
        weigh(0, 1, 3, 6, 2, 4, -1, 4, *ys, 1)
    for y in (-4, 11):
        weigh(0, 0, 3, 6, 2, 4, 0, 3, y, y, 1)
    loop(0, 5, start0)
    loop(11, 16, start0)
    loop(1, 5, start0b)
    loop(11, 15, start0b)
    half_sweep(0, 1, b0, r0, -2, 5, -3, 10)
    half_sweep(0, 0, r0, b0, -1, 4, -2, 9)
    half_sweep(0, 1, b0, r0, -1, 4, -1, 8)

    def rest0(y, c):
        qs = list(range(4))
        red = residual(0, 0, r0, b0, qs, y)
        black = residual(0, 1, b0, r0, qs, y)
        for q in qs:
            s0[q, y] = red[q] + black[q]
            p0[q + 3, y + 6] = b0[q + 3, y + 6]
        return c

    loop(0, 8, rest0)
    coarse1(lambda z, y: s0[z, y], c1f)
    put1("f1", "c1f", ring, None, None, 4)
    received("k2")
    total = jnp.zeros(T8, F32)
    for n in range(8):
        total = total + open2(m2k, 4, n // 4, n // 2 % 2, n % 2)
    m3k, m3f = B["m3k"], B["m3f"]
    m3k[gy] = total * 0.125
    for dy in (4, -4, 3, -3, 2, -2, 1, -1):
        put("k2x", m2k.at[4], m2k.at[4 - dy], 8, 0, dy)
    for dy in line:
        put("k3", m3k.at[gy], m3k.at[gy], 1, 0, dy)

    received("k1")
    k1 = B["k1"]
    for side, q_cut, y_cut in ((gz == 0, (0, 4), None), (gz == 1, (0, 2), None), (gz == nz - 1, (6, 10), None), (gz == nz - 2, (8, 10), None),
                               (gy == 0, None, (0, 8)), (gy == 1, None, (0, 4)), (gy == ny - 1, None, (12, 20)), (gy == ny - 2, None, (16, 20))):
        @pl.when(side)
        def _(q_cut=q_cut, y_cut=y_cut):
            for q in range(*(q_cut or (0, 10))):
                blank("c1k", (q, slice(*(y_cut or (0, 20)))))

    def open1(y, c):
        for q in range(10):
            v = c1k[q, y]
            k1[0, q, y] = v
            k1[1, q, y] = pltpu.roll(v, 127, 1)
        return c

    loop(0, 20, open1)
    weigh(1, 0, 4, 8, 3, 6, -3, 4, -6, 9, 2)
    weigh(1, 1, 4, 8, 3, 6, -3, 4, -5, 8, 2)

    k2, w2, d2, g2, r2, b2, p2 = (B[n] for n in ("k2", "w2", "d2", "g2", "r2", "b2", "p2"))

    def fill2(d, c):
        there = gy + d - 4
        inside = jnp.where((there >= 0) & (there < ny), 1.0, 0.0)
        for y2 in range(2):
            for zp in range(2):
                for colour in range(2):
                    k2[colour, 2 * d + y2 + 1, zp] = open2(m2k, d, y2, zp, (colour + y2 + zp) % 2) * inside
        return c


    def near2(ref, row, p, zp, colour, edge):
        o, oz = ref[row, zp], ref[row, 1 - zp]
        if (colour + p + zp) % 2 == 0:
            x = pltpu.roll(o, 1, 1)
            x = jnp.where(lane == 0, 0.0, x) if edge else x
        else:
            x = pltpu.roll(o, 127, 1)
            x = jnp.where(lane == 127, 0.0, x) if edge else x
        if zp == 0:
            z = pltpu.roll(oz, 1, 0)
            z = jnp.where(sub == 0, 0.0, z) if edge else z
        else:
            z = pltpu.roll(oz, 7, 0)
            z = jnp.where(sub == 7, 0.0, z) if edge else z
        return (oz, z, ref[row - 1, zp], ref[row + 1, zp], o, x)

    def weigh2(d, c):
        for p in range(2):
            for zp in range(2):
                for colour in range(2):
                    row = 2 * d + p
                    inverse, ws = weights(k2[colour, row + 1, zp], near2(k2.at[1 - colour], row + 1, p, zp, colour, True))
                    d2[colour, row, zp] = inverse
                    for i in range(6):
                        w2[colour, i, row, zp] = ws[i]
        return c


    def fresh2(d, p, zp, colour, other):
        row = 2 * d + p
        u = near2(other, row + 1, p, zp, colour, False)
        acc = g2[colour, row, zp]
        for i in range(6):
            acc = acc + w2[colour, i, row, zp] * u[i]
        return acc

    def half_sweep2(colour, target, other, first, last):
        def rows(ds):
            at = [(d, p, zp) for d in ds for p in range(2) for zp in range(2)]
            values = [fresh2(d, p, zp, colour, other) for d, p, zp in at]
            for (d, p, zp), v in zip(at, values):
                target[2 * d + p + 1, zp] = v

        def body(i, c):
            rows([3 * i + first + n for n in range(3)])
            return c

        steps = (last + 1 - first) // 3
        lax.fori_loop(0, steps, body, 0)
        if first + 3 * steps <= last:
            rows(range(first + 3 * steps, last + 1))

    received("f1")
    d1, g1, r1, b1, p1, s1 = (B[n] for n in ("d1", "g1", "r1", "b1", "p1", "s1"))

    def start1(q0, q1, y0, y1, write):
        def body(y, c):
            for q in range(q0, q1 + 1):
                v = c1f[q + 4, y + 8]
                red = v * (4.0 * d1[0, q + 3, y + 6])
                g1[0, q + 3, y + 6] = red
                if write:
                    r1[q + 4, y + 8] = red
                g1[1, q + 3, y + 6] = pltpu.roll(v, 127, 1) * (4.0 * d1[1, q + 3, y + 6])
            return c

        loop(y0, y1 + 1, body)

    start1(-2, 3, -4, 7, True)
    half_sweep(1, 1, b1, r1, -2, 3, -3, 6)
    half_sweep(1, 0, r1, b1, -1, 2, -2, 5)
    half_sweep(1, 1, b1, r1, -1, 2, -1, 4)

    def rest1(y, c):
        qs = [0, 1]
        red = residual(1, 0, r1, b1, qs, y)
        black = residual(1, 1, b1, r1, qs, y)
        for q in qs:
            s1[q, y] = red[q] + black[q]
        return c

    loop(0, 4, rest1)
    m2f[4, gz] = coarse2(lambda q, y: s1[q, y])
    for dz, dy in patch:
        put("f2", m2f.at[4, gz], m2f.at[4 - dy, gz], 1, dz, dy)
    put1("f1x", "c1f", far + knights, (1, 2), (1, 1), 4)
    p1c = B["p1c"]
    for q in range(2):
        for y in range(2):
            p1c[q + 4, y + 4] = jnp.where(lane % 2 == 0, b1[q + 4, 2 * y + 8], pltpu.roll(b1[q + 4, 2 * y + 9], 1, 1))
    put1("u1", "p1c", around, (2, 2), (1, 1), 2)
    received("k2x")
    loop(0, 9, fill2, 3)
    loop(0, 9, weigh2)

    received("k3")
    k3, w3, d3, g3, r3, b3, e3 = (B[n] for n in ("k3", "w3", "d3", "g3", "r3", "b3", "e3"))
    even3 = (lane + sub) % 2 == 0
    for m in range(16):
        lo, hi = m3k[2 * m], m3k[2 * m + 1]
        k3[0, m + 1] = jnp.where(even3, lo, hi)
        k3[1, m + 1] = jnp.where(even3, hi, lo)

    def near3(ref, m, colour, edge):
        o = ref[m + 1]
        low = even3 if colour == 0 else jnp.logical_not(even3)
        zm, zp, xm, xp = pltpu.roll(o, 1, 0), pltpu.roll(o, 7, 0), pltpu.roll(o, 1, 1), pltpu.roll(o, 127, 1)
        if edge:
            zm, zp = jnp.where(sub == 0, 0.0, zm), jnp.where(sub == 7, 0.0, zp)
            xm, xp = jnp.where(lane == 0, 0.0, xm), jnp.where(lane == 127, 0.0, xp)
        return (o, jnp.where(low, ref[m], ref[m + 2]), zm, zp, xm, xp)

    def weigh3(m, c):
        for colour in range(2):
            inverse, ws = weights(k3[colour, m + 1], near3(k3.at[1 - colour], m, colour, True))
            d3[colour, m] = inverse * 64.0
            for i in range(6):
                w3[colour, i, m] = ws[i]
        return c

    loop(0, 16, weigh3)

    received("f2")

    def start2(d0_, d1_, write):
        def body(d, c):
            for y2 in range(2):
                for zp in range(2):
                    for colour in range(2):
                        row = 2 * d + y2
                        v = open2(m2f, d, y2, zp, (colour + y2 + zp) % 2) * (16.0 * d2[colour, row, zp])
                        g2[colour, row, zp] = v
                        if write and colour == 0:
                            r2[row + 1, zp] = v
            return c

        loop(d0_, d1_ + 1, body)

    start2(2, 6, True)
    half_sweep2(1, b2, r2, 2, 6)
    half_sweep2(0, r2, b2, 3, 5)
    half_sweep2(1, b2, r2, 3, 5)
    total = jnp.zeros(T8, F32)
    for p in range(2):
        for zp in range(2):
            for colour in range(2):
                own, other = (r2, b2) if colour == 0 else (b2, r2)
                v = fresh2(4, p, zp, colour, other) - own[9 + p, zp]
                total = total + v / (d2[colour, 8 + p, zp] * 16.0)
            p2[9 + p, zp] = b2[9 + p, zp]
    m3f[gy] = total * 0.125
    for dy in line:
        put("f3", m3f.at[gy], m3f.at[gy], 1, 0, dy)
    for dy in (4, -4, 3, -3):
        put("f2x", m2f.at[4], m2f.at[4 - dy], 8, 0, dy)
    for dy in range(-4, 5):
        if dy:
            put("u2", p2.at[pl.ds(9, 2)], p2.at[pl.ds(9 - 2 * dy, 2)], 4, 0, dy)

    halo0("u0", [("p0", 3, 6, None, 5)])

    received("f1x")
    start1(-3, 4, -6, 9, False)

    received("f3")
    for m in range(16):
        lo, hi = m3f[2 * m], m3f[2 * m + 1]
        red = jnp.where(even3, lo, hi) * d3[0, m]
        g3[0, m] = red
        r3[m + 1] = red
        g3[1, m] = jnp.where(even3, hi, lo) * d3[1, m]

    def half_sweep3(colour, target, other):
        for m in range(16):
            u = near3(other, m, colour, False)
            acc = g3[colour, m]
            for i in range(6):
                acc = acc + w3[colour, i, m] * u[i]
            target[m + 1] = acc

    half_sweep3(1, b3, r3)

    def sweep3(s, c):
        half_sweep3(0, r3, b3)
        half_sweep3(1, b3, r3)
        return c

    lax.fori_loop(0, 11, sweep3, 0)
    for m in range(16):
        red, black = r3[m + 1], b3[m + 1]
        e3[2 * m + 4] = jnp.where(even3, red, black)
        e3[2 * m + 5] = jnp.where(even3, black, red)

    received("f2x")
    start2(0, 1, False)
    start2(7, 8, False)
    received("u2")
    finished("u2")

    def up2(d, c):
        e = e3[gy + d]
        for p in range(2):
            for zp in range(2):
                p2[2 * d + p + 1, zp] = p2[2 * d + p + 1, zp] + e
        return c

    loop(0, 9, up2, 3)
    half_sweep2(0, r2, p2, 0, 8)
    half_sweep2(1, p2, r2, 1, 7)
    half_sweep2(0, r2, p2, 1, 7)
    half_sweep2(1, p2, r2, 2, 6)

    e2v, e2x = B["e2v"], B["e2x"]

    def store2(d, c):
        for p in range(2):
            for zp in range(2):
                for colour in range(2):
                    ref = r2 if colour == 0 else p2
                    e2v[2 * (d - 2) + p, zp, (colour + p + zp) % 2, pl.ds(8, 8), :] = ref[2 * d + p + 1, zp]
        return c

    loop(2, 7, store2, 5)
    spread = 16 * sub + lane // 8

    def spread2(y2, c):
        for z2 in range(-4, 6):
            parts = []
            for j in range(2):
                row = e2v[y2, z2 % 2, j, pl.ds(8 + gz + z2 // 2, 1), :]
                parts.append(jnp.take_along_axis(jnp.broadcast_to(row, T8), spread, axis=1))
            e2x[z2 + 4, y2] = jnp.where((lane // 4) % 2 == 0, parts[0], parts[1])
        return c

    loop(0, 10, spread2)

    received("u1")

    def up1(y2, c):
        for q in range(10):
            e = e2x[q, y2]
            for p in range(2):
                p1[q, 2 * y2 + p] = (pltpu.roll(p1c[q, y2], 127, 1) if p else p1c[q, y2]) + e
        return c

    loop(0, 10, up1)
    half_sweep(1, 0, r1, p1, -3, 4, -6, 9)
    half_sweep(1, 1, p1, r1, -3, 4, -5, 8)
    half_sweep(1, 0, r1, p1, -2, 3, -4, 7)
    half_sweep(1, 1, p1, r1, -2, 3, -3, 6)

    received("u0")
    finished("u0")

    def up0(y1, c):
        even = (lane // 2 + y1) & 1 == 0
        for q in range(-2, 4):
            red, black = r1[q + 4, y1 + 8], p1[q + 4, y1 + 8]
            for p in range(2):
                z1 = 2 * q + p
                if -3 <= z1 <= 6:
                    e = jnp.where(even, red, black) if p == 0 else jnp.where(even, black, red)
                    e = jnp.where(lane % 2 == 0, e, pltpu.roll(e, 1, 1))
                    for i in range(2):
                        p0[z1 + 3, 2 * y1 + i + 6] = p0[z1 + 3, 2 * y1 + i + 6] + e
        return c

    loop(-3, 7, up0)
    half_sweep(0, 0, r0, p0, -2, 5, -4, 11)
    half_sweep(0, 1, p0, r0, -2, 5, -3, 10)
    half_sweep(0, 0, r0, p0, -1, 4, -2, 9)
    half_sweep(0, 1, p0, r0, -1, 4, -1, 8)

    out_u, out_r = u_out.reshape(512, 128), r_out.reshape(512, 128)

    def finish(y, c):
        even = (lane + y) & 1 == 0
        qs = list(range(4))
        res_red = residual(0, 0, r0, p0, qs, y)
        res_black = residual(0, 1, p0, r0, qs, y)
        for q in qs:
            red, black = r0[q + 3, y + 6], p0[q + 3, y + 6]
            lo, hi = pl.ds(2 * q * 64 + y, 8, stride=8), pl.ds((2 * q + 1) * 64 + y, 8, stride=8)
            out_u[lo, :] = jnp.where(even, red, black)
            out_u[hi, :] = jnp.where(even, black, red)
            out_r[lo, :] = jnp.where(even, res_red[q], res_black[q])
            out_r[hi, :] = jnp.where(even, res_black[q], res_red[q])
        return c

    loop(0, 8, finish)
    for group in GROUPS:
        if group not in ("u0", "u2"):
            finished(group)


def solution(mesh):
    nz, ny = mesh.shape["gz"], mesh.shape["gy"]

    def on_device(right_side, coefficient):
        depth, rows, width = right_side.shape
        out = jax.ShapeDtypeStruct((depth, width // 128, rows, 128), F32)

        def tiles(array):
            return array.reshape(depth, rows, width // 128, 128).transpose(0, 2, 1, 3)

        def whole(array):
            return array.transpose(0, 2, 1, 3).reshape(depth, rows, width)

        def body(*refs):
            kernel(nz, ny, *refs)

        scratch = []
        for name, shape in BUFFERS.items():
            if name in ("stage_f", "stage_k"):
                scratch.append(pltpu.VMEM((8, 8, 8, 128), F32))
            elif name == "e2v":
                scratch.append(pltpu.VMEM((10, 2, 2, 24, 128), F32))
            else:
                scratch.append(pltpu.VMEM(shape + T8, F32))
        correction, residual = pl.pallas_call(
            body,
            out_shape=(out, out),
            in_specs=[pl.BlockSpec(memory_space=pltpu.HBM)] * 2,
            out_specs=[pl.BlockSpec(memory_space=pltpu.VMEM)] * 2,
            scratch_shapes=scratch
            + [pltpu.SemaphoreType.DMA((2,)), pltpu.SemaphoreType.DMA((len(GROUPS),)), pltpu.SemaphoreType.DMA((len(GROUPS),))],
            compiler_params=pltpu.CompilerParams(collective_id=0, has_side_effects=True, vmem_limit_bytes=40 * 1024 * 1024),
            name="vcycle",
        )(tiles(right_side), tiles(coefficient))
        return whole(correction), whole(residual)

    placed = (P("gz", "gy", None), P("gz", "gy", None))
    return jax.shard_map(on_device, mesh=mesh, in_specs=placed, out_specs=placed, check_vma=False)
```

```python
import jax
import jax.numpy as jnp
from jax import lax
from jax.experimental import pallas as pl
from jax.experimental.pallas import tpu as pltpu
from jax.sharding import PartitionSpec as P

MESH = pl.DeviceIdType.MESH
F32 = jnp.float32
T8 = (8, 128)

BUFFERS = dict(
    stage_f=(8, 8), stage_k=(8, 8),
    k0=(2, 10, 20), f0=(2, 8, 16), w0=(2, 6, 8, 16), d0=(2, 8, 16), g0=(2, 8, 16), r0=(10, 20), b0=(10, 20), p0=(10, 20),
    s0=(4, 8),
    c1k=(10, 20), c1f=(10, 20), k1=(2, 10, 20), w1=(2, 6, 8, 16), d1=(2, 8, 16), g1=(2, 8, 16), r1=(10, 20), b1=(10, 20), p1=(10, 20),
    s1=(2, 4), p1c=(10, 10),
    m2k=(9, 8), m2f=(9, 8), k2=(2, 20, 2), w2=(2, 6, 18, 2), d2=(2, 18, 2), g2=(2, 18, 2), r2=(20, 2), b2=(20, 2), p2=(20, 2),
    e2v=(10, 2, 2, 3), e2x=(10, 10),
    m3k=(32,), m3f=(32,), k3=(2, 18), w3=(2, 6, 16), d3=(2, 16), g3=(2, 16), r3=(18,), b3=(18,), e3=(40,),
)
GROUPS = ("h0z", "h0", "k1", "k2", "k2x", "f1", "f1x", "u0", "u1", "k3", "f2", "f2x", "u2", "f3")


def iota(dim):
    return lax.broadcasted_iota(jnp.int32, T8, dim)


def nearest(d, n, size):
    if d == 0:
        return 0, 0, size
    if d > 0:
        return size - n, -d * size + size - n, n
    return 0, -d * size, n


def loop(first, end, body, rows=2):
    steps = (end - first) // rows

    def shifted(i, c):
        for n in range(rows):
            body(i * rows + (first + n), c)
        return c

    lax.fori_loop(0, steps, shifted, 0)
    for y in range(first + steps * rows, end):
        body(jnp.int32(y), 0)


def kernel(nz, ny, f_in, k_in, u_out, r_out, *scratch):
    B = dict(zip(BUFFERS, scratch))
    in_sem, send_sem, recv_sem = scratch[len(BUFFERS):]
    gz, gy = lax.axis_index("gz"), lax.axis_index("gy")
    lane, sub = iota(1), iota(0)
    sent = dict.fromkeys(GROUPS, 0)

    def device(dz, dy):
        return (lax.rem(gz + (dz + nz) % nz, nz), lax.rem(gy + (dy + ny) % ny, ny))

    def wait_bytes(sem, n):
        view = B["w0"].reshape(1536, 8, 128).at[pl.ds(0, n)]
        pltpu.make_async_copy(view, view, sem).wait()

    pltpu.make_async_copy(k_in, B["stage_k"], in_sem.at[0]).start()
    pltpu.make_async_copy(f_in, B["stage_f"], in_sem.at[1]).start()

    ring = [(0, 1), (0, -1), (1, 1), (1, -1), (-1, 1), (-1, -1), (1, 0), (-1, 0)]
    far = [(2, 0), (-2, 0), (0, 2), (0, -2)]
    knights = [(a, b) for a in (-2, -1, 1, 2) for b in (-2, -1, 1, 2) if abs(a) != abs(b)]
    around = ring + far + knights
    line = sorted(range(1, ny), key=lambda b: -min(b, ny - b))
    patch = [(a, b) for b in (2, -2, 1, -1, 0) for a in range(nz) if (a, b) != (0, 0)]
    everyone = patch + [(0, b) for b in line if 2 < b < ny - 2]
    barrier = pltpu.get_barrier_semaphore()
    for dz, dy in everyone:
        pl.semaphore_signal(barrier, inc=1, device_id=device(dz, dy), device_id_type=MESH)

    def put(group, src, dst, n, dz, dy):
        i = GROUPS.index(group)
        sent[group] += n
        pltpu.make_async_remote_copy(
            src_ref=src, dst_ref=dst, send_sem=send_sem.at[i], recv_sem=recv_sem.at[i],
            device_id=device(dz, dy), device_id_type=MESH,
        ).start()

    def received(group):
        wait_bytes(recv_sem.at[GROUPS.index(group)], sent[group])

    def finished(group):
        wait_bytes(send_sem.at[GROUPS.index(group)], sent[group])

    def packed(stage, dst, oq, oy):
        rows = B[stage].reshape(512, 128)
        target = B[dst]

        def body(y, c):
            even = (lane + y) & 1 == 0
            for q in range(4):
                lo = rows[pl.ds(2 * q * 64 + y, 8, stride=8), :]
                hi = rows[pl.ds((2 * q + 1) * 64 + y, 8, stride=8), :]
                target[0, q + oq, y + oy] = jnp.where(even, lo, hi)
                target[1, q + oq, y + oy] = jnp.where(even, hi, lo)
            return c

        loop(0, 8, body, 4)

    wait_bytes(in_sem.at[0], 64)
    packed("stage_k", "k0", 3, 6)
    wait_bytes(in_sem.at[1], 64)
    packed("stage_f", "f0", 2, 4)
    pl.semaphore_wait(barrier, len(everyone))

    covered = {}

    def put0(group, name, oq, oy, colour, dz, dy, nq, nyy, skip_q=0):
        sq, tq, lq = nearest(dz, nq, 4)
        sy, ty, ly = nearest(dy, nyy, 8)
        if skip_q:
            lq = nq - skip_q
            if dz < 0:
                sq, tq = sq + skip_q, tq + skip_q
        if lq <= 0 or ly <= 0:
            return
        ref = B[name] if colour is None else B[name].at[colour]
        covered.setdefault((name, colour), set()).update((tq + i + oq, ty + j + oy) for i in range(lq) for j in range(ly))
        put(group, ref.at[pl.ds(sq + oq, lq), pl.ds(sy + oy, ly)], ref.at[pl.ds(tq + oq, lq), pl.ds(ty + oy, ly)], lq * ly, dz, dy)

    def halo0(group, fields):
        for dz, dy in ((0, 1), (0, -1)):
            for name, oq, oy, colour, depth in fields:
                put0(group, name, oq, oy, colour, dz, dy, 0, depth)
        for dz, dy in ((1, 0), (-1, 0)):
            for name, oq, oy, colour, depth in fields:
                put0(group + "z" * (group == "h0"), name, oq, oy, colour, dz, dy, (depth + 1) // 2, 0)
        for dz, dy in ((1, 1), (1, -1), (-1, 1), (-1, -1)):
            for name, oq, oy, colour, depth in fields:
                put0(group, name, oq, oy, colour, dz, dy, 1, depth - 1)
                put0(group, name, oq, oy, colour, dz, dy, 2, depth - 3, 1)

    halo0("h0", [("k0", 3, 6, 1, 5), ("k0", 3, 6, 0, 4), ("f0", 2, 4, 0, 4), ("f0", 2, 4, 1, 3)])

    def clear(name, index, own, got):
        nq, nyy = BUFFERS[name][-2:]
        have = got | {(own[0] + i, own[1] + j) for i in range(own[2]) for j in range(own[3])}
        for q in range(nq):
            y = 0
            while y < nyy:
                end = y
                while end < nyy and (q, end) not in have:
                    end += 1
                if end > y:
                    B[name][index + (q, slice(y, end))] = jnp.zeros((end - y,) + T8, F32)
                y = end + 1

    def put1(group, name, which, far_depth, knight_depth, rows, dry=False):
        ref, oy = B[name], 2 * rows
        for dz, dy in which:
            nq, nr = (2, rows) if (dz, dy) in ring else knight_depth if (dz, dy) in knights else far_depth
            sq, tq, lq = nearest(dz, nq, 2)
            sy, ty, ly = nearest(dy, nr, rows)
            if dry:
                covered.setdefault(name, set()).update((tq + i + 4, ty + j + oy) for i in range(lq) for j in range(ly))
            else:
                put(group, ref.at[pl.ds(sq + 4, lq), pl.ds(sy + oy, ly)], ref.at[pl.ds(tq + 4, lq), pl.ds(ty + oy, ly)], lq * ly, dz, dy)

    def coarse1(read, target):
        def body(y1, c):
            even = (lane // 2 + y1) & 1 == 0
            cols = []
            for z1 in range(4):
                t = read(z1, 2 * y1) + read(z1, 2 * y1 + 1)
                cols.append((t + pltpu.roll(t, 127, 1)) * 0.125)
            for q in range(2):
                lo, hi = cols[2 * q], cols[2 * q + 1]
                red, black = jnp.where(even, lo, hi), jnp.where(even, hi, lo)
                target[q + 4, y1 + 8] = jnp.where(lane % 2 == 0, red, pltpu.roll(black, 1, 1))
            return c

        loop(0, 4, body, 4)

    def coarse2(read):
        out = jnp.zeros(T8, F32)
        for y2 in range(2):
            for z2 in range(2):
                t = read(z2, 2 * y2) + read(z2, 2 * y2 + 1)
                t = (t + pltpu.roll(t, 126, 1)) * 0.125
                for j in range(2):
                    v = jnp.take_along_axis(t, (lane % 16) * 8 + 4 * j, axis=1)
                    v = jnp.sum(jnp.where(lane // 16 == sub, v, 0.0), axis=0, keepdims=True)
                    out = jnp.where(sub == y2 * 4 + z2 * 2 + j, jnp.broadcast_to(v, T8), out)
        return out

    k0, c1k, c1f = B["k0"], B["c1k"], B["c1f"]
    coarse1(lambda z, y: k0[0, z + 3, y + 6] + k0[1, z + 3, y + 6], c1k)
    m2k, m2f = B["m2k"], B["m2f"]

    def both1(q, y):
        v = c1k[q + 4, y + 8]
        return v + pltpu.roll(v, 127, 1)

    m2k[4, gz] = coarse2(both1)
    for dz in range(1, nz):
        put("k2", m2k.at[4, gz], m2k.at[4, gz], 1, dz, 0)

    own0, own1 = (3, 6, 4, 8), (4, 8, 2, 4)
    for colour in range(2):
        clear("k0", (colour,), own0, covered["k0", colour])
        clear("f0", (colour,), (2, 4, 4, 8), covered["f0", colour])
    clear("p0", (), own0, covered["k0", 1])
    put1("", "c1k", around, (2, 3), (1, 2), 4, True)
    put1("", "c1f", around, (1, 2), (1, 1), 4, True)
    put1("", "p1c", around, (2, 2), (1, 1), 2, True)
    clear("c1k", (), own1, covered["c1k"])
    clear("c1f", (), own1, covered["c1f"])
    clear("p1c", (), (4, 4, 2, 2), covered["p1c"])

    def wipe(i, c):
        for name in ("r0", "b0", "r1", "b1"):
            B[name][i] = jnp.zeros((20,) + T8, F32)
        B["e2v"][i] = jnp.zeros((2, 2, 24, 128), F32)
        return c

    lax.fori_loop(0, 10, wipe, 0)
    for row in (0, 19):
        for colour in range(2):
            B["k2"][colour, row] = jnp.zeros((2,) + T8, F32)
        B["p2"][row] = jnp.zeros((2,) + T8, F32)
    for name in ("r2", "b2"):
        B[name][...] = jnp.zeros((20, 2) + T8, F32)
    for m in (0, 17):
        for colour in range(2):
            B["k3"][colour, m] = jnp.zeros(T8, F32)
        B["r3"][m] = jnp.zeros(T8, F32)
        B["b3"][m] = jnp.zeros(T8, F32)
    for m in (0, 36):
        B["e3"][m:m + 4] = jnp.zeros((4,) + T8, F32)

    def open2(ref, d, y2, zp, j):
        return ref.reshape(576, 128)[pl.ds(d * 64 + y2 * 4 + zp * 2 + j, 8, stride=8), :]

    def shifts(v, st, edge):
        a = pltpu.roll(v, st, 1)
        m = jnp.where(lane < st, pltpu.roll(a, 1, 0), a)
        a = pltpu.roll(v, 128 - st, 1)
        p = jnp.where(lane >= 128 - st, pltpu.roll(a, 7, 0), a)
        if edge:
            m = jnp.where((lane < st) & (sub == 0), 0.0, m)
            p = jnp.where((lane >= 128 - st) & (sub == 7), 0.0, p)
        return m, p

    def row_neighbours(ref, qs, y, colour, st, edge):
        at = {q: ref[q, y] for q in range(qs[0] - 1, qs[-1] + 2)}
        low = (lane // st + y + colour) & 1 == 0
        out = []
        for q in qs:
            o = at[q]
            m, p = shifts(o, st, edge)
            out.append((o, jnp.where(low, at[q - 1], at[q + 1]), ref[q, y - 1], ref[q, y + 1], m, p))
        return out

    def weights(own, others):
        diag = 0.5 * (6.0 * own + sum(others[1:], others[0]))
        inverse = jnp.where(own > 0.0, 1.0 / diag, 0.0)
        return inverse, [jnp.where(k > 0.0, 0.5 * (own + k) * inverse, 0.0) for k in others]

    def weigh(level, colour, oq, oy, wq, wy, q0, q1, y0, y1, st):
        k, w, d = B["k%d" % level], B["w%d" % level], B["d%d" % level]

        def body(y, c):
            qs = [q + oq for q in range(q0, q1 + 1)]
            near = row_neighbours(k.at[1 - colour], qs, y + oy, colour, st, True)
            for q, others in zip(qs, near):
                inverse, ws = weights(k[colour, q, y + oy], others)
                d[colour, q - oq + wq, y + wy] = inverse
                for i in range(6):
                    w[colour, i, q - oq + wq, y + wy] = ws[i]
            return c

        loop(y0, y1 + 1, body)

    def fresh(level, colour, qs, y, other, oq, oy, wq, wy, st):
        w, g = B["w%d" % level], B["g%d" % level]
        near = row_neighbours(other, [q + oq for q in qs], y + oy, colour, st, False)
        out = []
        for q, u in zip(qs, near):
            at = (q + wq, y + wy)
            acc = g[(colour,) + at]
            for i in range(6):
                acc = acc + w[(colour, i) + at] * u[i]
            out.append(acc)
        return out

    def half_sweep(level, colour, target, other, q0, q1, y0, y1):
        oq, oy, wq, wy, st = PLACE[level]

        qs = list(range(q0, q1 + 1))

        def rows(ys):
            values = [fresh(level, colour, qs, y, other, oq, oy, wq, wy, st) for y in ys]
            for y, row in zip(ys, values):
                for q, v in zip(qs, row):
                    target[q + oq, y + oy] = v

        def body(i, c):
            rows([4 * i + y0 + n for n in range(4)])
            return c

        steps = (y1 + 1 - y0) // 4
        lax.fori_loop(0, steps, body, 0)
        if y0 + 4 * steps <= y1:
            rows(range(y0 + 4 * steps, y1 + 1))

    def residual(level, colour, own, other, qs, y):
        oq, oy, wq, wy, st = PLACE[level]
        d = B["d%d" % level]
        new = fresh(level, colour, qs, y, other, oq, oy, wq, wy, st)
        return [(v - own[q + oq, y + oy]) / (d[colour, q + wq, y + wy] * 4.0**level) for q, v in zip(qs, new)]

    PLACE = {0: (3, 6, 2, 4, 1), 1: (4, 8, 3, 6, 2)}

    def blank(name, at):
        ref = B[name]
        shape = BUFFERS[name]
        size = [len(range(*a.indices(n))) if isinstance(a, slice) else None for a, n in zip(at, shape)]
        ref[at] = jnp.zeros(tuple(s for s in size if s is not None) + T8, F32)

    def blank0(side, qs, spans):
        @pl.when(side)
        def _():
            for colour in range(2):
                for q in qs:
                    for span in spans:
                        blank("k0", (colour, q, slice(*span)))

    f0, d0, g0, r0, b0, p0, s0 = (B[n] for n in ("f0", "d0", "g0", "r0", "b0", "p0", "s0"))

    def start0(y, c):
        for q in range(8):
            red = f0[0, q, y] * d0[0, q, y]
            g0[0, q, y] = red
            r0[q + 1, y + 2] = red
        return c


    def start0b(y, c):
        for q in range(8):
            g0[1, q, y] = f0[1, q, y] * d0[1, q, y]
        return c

    received("h0z")
    blank0(gz == 0, range(0, 3), [(6, 14)])
    blank0(gz == nz - 1, range(7, 10), [(6, 14)])
    weigh(0, 0, 3, 6, 2, 4, -2, 5, 1, 6, 1)
    weigh(0, 1, 3, 6, 2, 4, -2, 5, 1, 6, 1)
    loop(5, 11, start0)
    loop(5, 11, start0b)
    put1("k1", "c1k", around, (2, 3), (1, 2), 4)
    received("h0")
    blank0(gz == 0, range(0, 3), [(0, 6), (14, 20)])
    blank0(gz == nz - 1, range(7, 10), [(0, 6), (14, 20)])
    blank0(gy == 0, range(10), [(0, 6)])
    blank0(gy == ny - 1, range(10), [(14, 20)])
    for ys in ((-1, 0), (7, 8)):
        weigh(0, 0, 3, 6, 2, 4, -2, 5, *ys, 1)
        weigh(0, 1, 3, 6, 2, 4, -2, 5, *ys, 1)
    for ys in ((-3, -2), (9, 10)):
        weigh(0, 0, 3, 6, 2, 4, -1, 4, *ys, 1)
        weigh(0, 1, 3, 6, 2, 4, -1, 4, *ys, 1)
    for y in (-4, 11):
        weigh(0, 0, 3, 6, 2, 4, 0, 3, y, y, 1)
    loop(0, 5, start0)
    loop(11, 16, start0)
    loop(1, 5, start0b)
    loop(11, 15, start0b)
    half_sweep(0, 1, b0, r0, -2, 5, -3, 10)
    half_sweep(0, 0, r0, b0, -1, 4, -2, 9)
    half_sweep(0, 1, b0, r0, -1, 4, -1, 8)

    def rest0(y, c):
        qs = list(range(4))
        red = residual(0, 0, r0, b0, qs, y)
        black = residual(0, 1, b0, r0, qs, y)
        for q in qs:
            s0[q, y] = red[q] + black[q]
            p0[q + 3, y + 6] = b0[q + 3, y + 6]
        return c

    loop(0, 8, rest0, 4)
    coarse1(lambda z, y: s0[z, y], c1f)
    put1("f1", "c1f", ring, None, None, 4)
    received("k2")
    total = jnp.zeros(T8, F32)
    for n in range(8):
        total = total + open2(m2k, 4, n // 4, n // 2 % 2, n % 2)
    m3k, m3f = B["m3k"], B["m3f"]
    m3k[gy] = total * 0.125
    for dy in (4, -4, 3, -3, 2, -2, 1, -1):
        put("k2x", m2k.at[4], m2k.at[4 - dy], 8, 0, dy)
    for dy in line:
        put("k3", m3k.at[gy], m3k.at[gy], 1, 0, dy)

    received("k1")
    k1 = B["k1"]
    for side, q_cut, y_cut in ((gz == 0, (0, 4), None), (gz == 1, (0, 2), None), (gz == nz - 1, (6, 10), None), (gz == nz - 2, (8, 10), None),
                               (gy == 0, None, (0, 8)), (gy == 1, None, (0, 4)), (gy == ny - 1, None, (12, 20)), (gy == ny - 2, None, (16, 20))):
        @pl.when(side)
        def _(q_cut=q_cut, y_cut=y_cut):
            for q in range(*(q_cut or (0, 10))):
                blank("c1k", (q, slice(*(y_cut or (0, 20)))))

    def open1(y, c):
        for q in range(10):
            v = c1k[q, y]
            k1[0, q, y] = v
            k1[1, q, y] = pltpu.roll(v, 127, 1)
        return c

    loop(0, 20, open1)
    weigh(1, 0, 4, 8, 3, 6, -3, 4, -6, 9, 2)
    weigh(1, 1, 4, 8, 3, 6, -3, 4, -5, 8, 2)

    k2, w2, d2, g2, r2, b2, p2 = (B[n] for n in ("k2", "w2", "d2", "g2", "r2", "b2", "p2"))

    def fill2(d, c):
        there = gy + d - 4
        inside = jnp.where((there >= 0) & (there < ny), 1.0, 0.0)
        for y2 in range(2):
            for zp in range(2):
                for colour in range(2):
                    k2[colour, 2 * d + y2 + 1, zp] = open2(m2k, d, y2, zp, (colour + y2 + zp) % 2) * inside
        return c


    def near2(ref, row, p, zp, colour, edge):
        o, oz = ref[row, zp], ref[row, 1 - zp]
        if (colour + p + zp) % 2 == 0:
            x = pltpu.roll(o, 1, 1)
            x = jnp.where(lane == 0, 0.0, x) if edge else x
        else:
            x = pltpu.roll(o, 127, 1)
            x = jnp.where(lane == 127, 0.0, x) if edge else x
        if zp == 0:
            z = pltpu.roll(oz, 1, 0)
            z = jnp.where(sub == 0, 0.0, z) if edge else z
        else:
            z = pltpu.roll(oz, 7, 0)
            z = jnp.where(sub == 7, 0.0, z) if edge else z
        return (oz, z, ref[row - 1, zp], ref[row + 1, zp], o, x)

    def weigh2(d, c):
        for p in range(2):
            for zp in range(2):
                for colour in range(2):
                    row = 2 * d + p
                    inverse, ws = weights(k2[colour, row + 1, zp], near2(k2.at[1 - colour], row + 1, p, zp, colour, True))
                    d2[colour, row, zp] = inverse
                    for i in range(6):
                        w2[colour, i, row, zp] = ws[i]
        return c


    def fresh2(d, p, zp, colour, other):
        row = 2 * d + p
        u = near2(other, row + 1, p, zp, colour, False)
        acc = g2[colour, row, zp]
        for i in range(6):
            acc = acc + w2[colour, i, row, zp] * u[i]
        return acc

    def half_sweep2(colour, target, other, first, last):
        def rows(ds):
            at = [(d, p, zp) for d in ds for p in range(2) for zp in range(2)]
            values = [fresh2(d, p, zp, colour, other) for d, p, zp in at]
            for (d, p, zp), v in zip(at, values):
                target[2 * d + p + 1, zp] = v

        def body(i, c):
            rows([4 * i + first + n for n in range(4)])
            return c

        steps = (last + 1 - first) // 4
        lax.fori_loop(0, steps, body, 0)
        if first + 4 * steps <= last:
            rows(range(first + 4 * steps, last + 1))

    received("f1")
    d1, g1, r1, b1, p1, s1 = (B[n] for n in ("d1", "g1", "r1", "b1", "p1", "s1"))

    def start1(q0, q1, y0, y1, write):
        def body(y, c):
            for q in range(q0, q1 + 1):
                v = c1f[q + 4, y + 8]
                red = v * (4.0 * d1[0, q + 3, y + 6])
                g1[0, q + 3, y + 6] = red
                if write:
                    r1[q + 4, y + 8] = red
                g1[1, q + 3, y + 6] = pltpu.roll(v, 127, 1) * (4.0 * d1[1, q + 3, y + 6])
            return c

        loop(y0, y1 + 1, body)

    start1(-2, 3, -4, 7, True)
    half_sweep(1, 1, b1, r1, -2, 3, -3, 6)
    half_sweep(1, 0, r1, b1, -1, 2, -2, 5)
    half_sweep(1, 1, b1, r1, -1, 2, -1, 4)

    def rest1(y, c):
        qs = [0, 1]
        red = residual(1, 0, r1, b1, qs, y)
        black = residual(1, 1, b1, r1, qs, y)
        for q in qs:
            s1[q, y] = red[q] + black[q]
        return c

    loop(0, 4, rest1, 4)
    m2f[4, gz] = coarse2(lambda q, y: s1[q, y])
    for dz, dy in patch:
        put("f2", m2f.at[4, gz], m2f.at[4 - dy, gz], 1, dz, dy)
    put1("f1x", "c1f", far + knights, (1, 2), (1, 1), 4)
    p1c = B["p1c"]
    for q in range(2):
        for y in range(2):
            p1c[q + 4, y + 4] = jnp.where(lane % 2 == 0, b1[q + 4, 2 * y + 8], pltpu.roll(b1[q + 4, 2 * y + 9], 1, 1))
    put1("u1", "p1c", around, (2, 2), (1, 1), 2)
    received("k2x")
    loop(0, 9, fill2, 3)
    loop(0, 9, weigh2)

    received("k3")
    k3, w3, d3, g3, r3, b3, e3 = (B[n] for n in ("k3", "w3", "d3", "g3", "r3", "b3", "e3"))
    even3 = (lane + sub) % 2 == 0
    for m in range(16):
        lo, hi = m3k[2 * m], m3k[2 * m + 1]
        k3[0, m + 1] = jnp.where(even3, lo, hi)
        k3[1, m + 1] = jnp.where(even3, hi, lo)

    def near3(ref, m, colour, edge):
        o = ref[m + 1]
        low = even3 if colour == 0 else jnp.logical_not(even3)
        zm, zp, xm, xp = pltpu.roll(o, 1, 0), pltpu.roll(o, 7, 0), pltpu.roll(o, 1, 1), pltpu.roll(o, 127, 1)
        if edge:
            zm, zp = jnp.where(sub == 0, 0.0, zm), jnp.where(sub == 7, 0.0, zp)
            xm, xp = jnp.where(lane == 0, 0.0, xm), jnp.where(lane == 127, 0.0, xp)
        return (o, jnp.where(low, ref[m], ref[m + 2]), zm, zp, xm, xp)

    def weigh3(m, c):
        for colour in range(2):
            inverse, ws = weights(k3[colour, m + 1], near3(k3.at[1 - colour], m, colour, True))
            d3[colour, m] = inverse * 64.0
            for i in range(6):
                w3[colour, i, m] = ws[i]
        return c

    loop(0, 16, weigh3)

    received("f2")

    def start2(d0_, d1_, write):
        def body(d, c):
            for y2 in range(2):
                for zp in range(2):
                    for colour in range(2):
                        row = 2 * d + y2
                        v = open2(m2f, d, y2, zp, (colour + y2 + zp) % 2) * (16.0 * d2[colour, row, zp])
                        g2[colour, row, zp] = v
                        if write and colour == 0:
                            r2[row + 1, zp] = v
            return c

        loop(d0_, d1_ + 1, body)

    start2(2, 6, True)
    half_sweep2(1, b2, r2, 2, 6)
    half_sweep2(0, r2, b2, 3, 5)
    half_sweep2(1, b2, r2, 3, 5)
    total = jnp.zeros(T8, F32)
    for p in range(2):
        for zp in range(2):
            for colour in range(2):
                own, other = (r2, b2) if colour == 0 else (b2, r2)
                v = fresh2(4, p, zp, colour, other) - own[9 + p, zp]
                total = total + v / (d2[colour, 8 + p, zp] * 16.0)
            p2[9 + p, zp] = b2[9 + p, zp]
    m3f[gy] = total * 0.125
    for dy in line:
        put("f3", m3f.at[gy], m3f.at[gy], 1, 0, dy)
    for dy in (4, -4, 3, -3):
        put("f2x", m2f.at[4], m2f.at[4 - dy], 8, 0, dy)
    for dy in range(-4, 5):
        if dy:
            put("u2", p2.at[pl.ds(9, 2)], p2.at[pl.ds(9 - 2 * dy, 2)], 4, 0, dy)

    halo0("u0", [("p0", 3, 6, None, 5)])

    received("f1x")
    start1(-3, 4, -6, 9, False)

    received("f3")
    for m in range(16):
        lo, hi = m3f[2 * m], m3f[2 * m + 1]
        red = jnp.where(even3, lo, hi) * d3[0, m]
        g3[0, m] = red
        r3[m + 1] = red
        g3[1, m] = jnp.where(even3, hi, lo) * d3[1, m]

    def half_sweep3(colour, target, other):
        for m in range(16):
            u = near3(other, m, colour, False)
            acc = g3[colour, m]
            for i in range(6):
                acc = acc + w3[colour, i, m] * u[i]
            target[m + 1] = acc

    half_sweep3(1, b3, r3)

    def sweep3(s, c):
        half_sweep3(0, r3, b3)
        half_sweep3(1, b3, r3)
        return c

    lax.fori_loop(0, 11, sweep3, 0)
    for m in range(16):
        red, black = r3[m + 1], b3[m + 1]
        e3[2 * m + 4] = jnp.where(even3, red, black)
        e3[2 * m + 5] = jnp.where(even3, black, red)

    received("f2x")
    start2(0, 1, False)
    start2(7, 8, False)
    received("u2")
    finished("u2")

    def up2(d, c):
        e = e3[gy + d]
        for p in range(2):
            for zp in range(2):
                p2[2 * d + p + 1, zp] = p2[2 * d + p + 1, zp] + e
        return c

    loop(0, 9, up2, 3)
    half_sweep2(0, r2, p2, 0, 8)
    half_sweep2(1, p2, r2, 1, 7)
    half_sweep2(0, r2, p2, 1, 7)
    half_sweep2(1, p2, r2, 2, 6)

    e2v, e2x = B["e2v"], B["e2x"]

    def store2(d, c):
        for p in range(2):
            for zp in range(2):
                for colour in range(2):
                    ref = r2 if colour == 0 else p2
                    e2v[2 * (d - 2) + p, zp, (colour + p + zp) % 2, pl.ds(8, 8), :] = ref[2 * d + p + 1, zp]
        return c

    loop(2, 7, store2, 5)
    spread = 16 * sub + lane // 8

    def spread2(y2, c):
        for z2 in range(-4, 6):
            parts = []
            for j in range(2):
                row = e2v[y2, z2 % 2, j, pl.ds(8 + gz + z2 // 2, 1), :]
                parts.append(jnp.take_along_axis(jnp.broadcast_to(row, T8), spread, axis=1))
            e2x[z2 + 4, y2] = jnp.where((lane // 4) % 2 == 0, parts[0], parts[1])
        return c

    loop(0, 10, spread2, 5)

    received("u1")

    def up1(y2, c):
        for q in range(10):
            e = e2x[q, y2]
            for p in range(2):
                p1[q, 2 * y2 + p] = (pltpu.roll(p1c[q, y2], 127, 1) if p else p1c[q, y2]) + e
        return c

    loop(0, 10, up1, 5)
    half_sweep(1, 0, r1, p1, -3, 4, -6, 9)
    half_sweep(1, 1, p1, r1, -3, 4, -5, 8)
    half_sweep(1, 0, r1, p1, -2, 3, -4, 7)
    half_sweep(1, 1, p1, r1, -2, 3, -3, 6)

    received("u0")
    finished("u0")

    def up0(y1, c):
        even = (lane // 2 + y1) & 1 == 0
        for q in range(-2, 4):
            red, black = r1[q + 4, y1 + 8], p1[q + 4, y1 + 8]
            for p in range(2):
                z1 = 2 * q + p
                if -3 <= z1 <= 6:
                    e = jnp.where(even, red, black) if p == 0 else jnp.where(even, black, red)
                    e = jnp.where(lane % 2 == 0, e, pltpu.roll(e, 1, 1))
                    for i in range(2):
                        p0[z1 + 3, 2 * y1 + i + 6] = p0[z1 + 3, 2 * y1 + i + 6] + e
        return c

    loop(-3, 7, up0, 5)
    half_sweep(0, 0, r0, p0, -2, 5, -4, 11)
    half_sweep(0, 1, p0, r0, -2, 5, -3, 10)
    half_sweep(0, 0, r0, p0, -1, 4, -2, 9)
    half_sweep(0, 1, p0, r0, -1, 4, -1, 8)

    out_u, out_r = u_out.reshape(512, 128), r_out.reshape(512, 128)

    def finish(y, c):
        even = (lane + y) & 1 == 0
        qs = list(range(4))
        res_red = residual(0, 0, r0, p0, qs, y)
        res_black = residual(0, 1, p0, r0, qs, y)
        for q in qs:
            red, black = r0[q + 3, y + 6], p0[q + 3, y + 6]
            lo, hi = pl.ds(2 * q * 64 + y, 8, stride=8), pl.ds((2 * q + 1) * 64 + y, 8, stride=8)
            out_u[lo, :] = jnp.where(even, red, black)
            out_u[hi, :] = jnp.where(even, black, red)
            out_r[lo, :] = jnp.where(even, res_red[q], res_black[q])
            out_r[hi, :] = jnp.where(even, res_black[q], res_red[q])
        return c

    loop(0, 8, finish, 4)
    for group in GROUPS:
        if group not in ("u0", "u2"):
            finished(group)


def solution(mesh):
    nz, ny = mesh.shape["gz"], mesh.shape["gy"]

    def on_device(right_side, coefficient):
        depth, rows, width = right_side.shape
        out = jax.ShapeDtypeStruct((depth, width // 128, rows, 128), F32)

        def tiles(array):
            return array.reshape(depth, rows, width // 128, 128).transpose(0, 2, 1, 3)

        def whole(array):
            return array.transpose(0, 2, 1, 3).reshape(depth, rows, width)

        def body(*refs):
            kernel(nz, ny, *refs)

        scratch = []
        for name, shape in BUFFERS.items():
            if name in ("stage_f", "stage_k"):
                scratch.append(pltpu.VMEM((8, 8, 8, 128), F32))
            elif name == "e2v":
                scratch.append(pltpu.VMEM((10, 2, 2, 24, 128), F32))
            else:
                scratch.append(pltpu.VMEM(shape + T8, F32))
        correction, residual = pl.pallas_call(
            body,
            out_shape=(out, out),
            in_specs=[pl.BlockSpec(memory_space=pltpu.HBM)] * 2,
            out_specs=[pl.BlockSpec(memory_space=pltpu.VMEM)] * 2,
            scratch_shapes=scratch
            + [pltpu.SemaphoreType.DMA((2,)), pltpu.SemaphoreType.DMA((len(GROUPS),)), pltpu.SemaphoreType.DMA((len(GROUPS),))],
            compiler_params=pltpu.CompilerParams(collective_id=0, has_side_effects=True, vmem_limit_bytes=40 * 1024 * 1024),
            name="vcycle",
        )(tiles(right_side), tiles(coefficient))
        return whole(correction), whole(residual)

    placed = (P("gz", "gy", None), P("gz", "gy", None))
    return jax.shard_map(on_device, mesh=mesh, in_specs=placed, out_specs=placed, check_vma=False)
```
